512 devices in a mesh: seq: 64 (over z, x_hi, core), dp: 8 (over y, x_lo).
Axes of the slice: x: 4 (x_hi: 2, x_lo: 2; x = x_hi * 2 + x_lo), y: 4, z: 16, core: 2. Of those that a mesh axis runs over, the one named last changes fastest.
Arguments:
- inputs: bfloat16 [8, 65536, 512], P('dp', 'seq'), may hold values from -16 to 16
- out_grad: bfloat16 [8, 65536, 512], P('dp', 'seq'), may hold values from -6 to 6
- first_factor: bfloat16 [128, 512, 512], P('seq', 'dp'), may hold values from -0.25 to 0.25
- second_factor: bfloat16 [512, 128, 128], P('seq', 'dp'), may hold values from -0.5 to 0.5
- gate_weight: bfloat16 [512, 512], P('seq', 'dp'), may hold values from -0.25 to 0.25
Outputs:
- grad_inputs: bfloat16 [8, 65536, 512], P('dp', 'seq')
- grad_first: float32 [128, 512, 512], P('seq', 'dp')
- grad_second: float32 [512, 128, 128], P('seq', 'dp')
- grad_gate: float32 [512, 512], P('seq', 'dp')
The draws below stay inside these ranges and needn't reach their ends.
All inputs are finite; a program needn't handle non-finite values.
Results may differ from the reference program's by a relative error of at most 0.006.
Values may be sent and summed in bfloat16 or wider, within the bound.
No kernel may reach another device: no remote copies, remote signals or barrier semaphores. Data moves between devices by JAX's collectives and lax.ppermute only.
A program may use at most 64 MiB of HBM per device.

```python
import jax
import jax.numpy as jnp
from jax import lax

D = 512
P1 = 512
P2 = 128
L = 65536
SEQS = 8


def spiked(entries, key, source, target, parts, factor):
    owner, partner = [(jnp.arange(entries.shape[dim]) // (entries.shape[dim] // parts)).reshape([-1 if axis == dim else 1 for axis in range(entries.ndim)]) for dim in (source, target)]
    chosen = jax.random.permutation(key, parts)[partner]
    strong = (owner == chosen) | (owner == (partner + parts // 2) % parts)
    return jnp.where(strong, factor * entries, entries)


def level_of(key, dims, shards, smallest, largest):
    def one(position, blocks):
        steps = jax.random.uniform(jax.random.fold_in(jax.random.fold_in(key, 6), position), (blocks,), jnp.float32, smallest / len(shards), largest / len(shards))
        return jnp.repeat(jnp.exp(steps), dims[position] // blocks).reshape((-1,) + (1,) * (len(dims) - position - 1))

    gain = one(*shards[0])
    for cut in shards[1:]:
        gain = gain * one(*cut)
    return gain


def centred(stream_key, shape, width, bound, split=(), dtype=jnp.bfloat16):
    array = jax.random.normal(stream_key, shape, jnp.float32) * width
    if len(split) > 0:
        array = level_of(stream_key, shape, split, -0.22, 0.18) * array
    return jnp.clip(array, min=-bound, max=bound).astype(dtype)


def gaussian_with(key, extent, width, most, split, heavy, kind=jnp.bfloat16):
    array = width * jax.random.normal(key, extent, jnp.float32)
    if split:
        array = array * level_of(key, extent, split, -0.22, 0.18)
    return jnp.clip(spiked(array, jax.random.fold_in(key, 3), *heavy), -most, most).astype(kind)


def setup_inputs(seed: int = 0) -> dict:
    keys = jax.random.split(jax.random.key(seed), 6)
    inputs = gaussian_with(keys[0], (SEQS, L, D), 1.0, 16.0, ((0, 8), (1, 64)), (1, 2, 64, 4.0))
    out_grad = gaussian_with(keys[1], (SEQS, L, D), 1.0, 6.0, ((0, 8), (1, 64)), (0, 2, 8, 2.0))
    first_factor = centred(keys[2], (P2, P1, P1), P1 ** -0.5, 0.25, ((0, 64), (1, 8)))
    second_factor = centred(keys[3], (P1, P2, P2), P2 ** -0.5, 0.5, ((0, 64), (1, 8)))
    gate_weight = centred(keys[4], (D, D), D ** -0.5, 0.25, ((0, 64), (1, 8)))
    return dict(inputs=inputs, out_grad=out_grad, first_factor=first_factor, second_factor=second_factor, gate_weight=gate_weight)


def reference(inputs, out_grad, first_factor, second_factor, gate_weight):
    first_wide = first_factor.astype(jnp.float32)
    second_wide = second_factor.astype(jnp.float32)

    def per_sequence(carry, pair):
        tokens, cot = pair
        blocked = tokens.reshape(P2, P1, D)
        cotangent = cot.reshape(P2, P1, D).astype(jnp.float32)
        gate = jax.nn.sigmoid(jnp.dot(tokens, gate_weight, preferred_element_type=jnp.float32)).reshape(P2, P1, D)
        mixed_one = jnp.einsum("ijk,ikd->ijd", first_wide, blocked.astype(jnp.float32)).astype(jnp.bfloat16)
        mixed_two = jnp.einsum("jpq,qjd->pjd", second_wide, mixed_one.astype(jnp.float32)).astype(jnp.bfloat16)
        mixed_grad = (cotangent * gate).astype(jnp.bfloat16)
        back_one = jnp.einsum("jpq,pjd->qjd", second_wide, mixed_grad.astype(jnp.float32)).astype(jnp.bfloat16)
        gate_delta = (cotangent * mixed_two.astype(jnp.float32) * gate * (1.0 - gate)).astype(jnp.bfloat16)
        flat_delta = gate_delta.reshape(L, D)
        grad_gate = carry[2] + jnp.dot(tokens.T, flat_delta, preferred_element_type=jnp.float32)
        gate_input = jnp.dot(flat_delta, gate_weight.T, preferred_element_type=jnp.float32).astype(jnp.bfloat16)
        grad_second = carry[1] + jnp.einsum("pjd,qjd->jpq", mixed_grad.astype(jnp.float32), mixed_one.astype(jnp.float32))
        grad_first = carry[0] + jnp.einsum("ijd,ikd->ijk", back_one.astype(jnp.float32), blocked.astype(jnp.float32))
        through = jnp.einsum("ijk,ijd->ikd", first_wide, back_one.astype(jnp.float32))
        grad_x = (through + gate_input.reshape(P2, P1, D).astype(jnp.float32)).astype(jnp.bfloat16).reshape(L, D)
        return (grad_first, grad_second, grad_gate), grad_x

    start = (jnp.zeros((P2, P1, P1), jnp.float32), jnp.zeros((P1, P2, P2), jnp.float32), jnp.zeros((D, D), jnp.float32))
    carry, grads = lax.scan(per_sequence, start, (inputs, out_grad))
    return grads, carry[0], carry[1], carry[2]
```

```python
import jax
import jax.numpy as jnp
from jax import lax
from jax.sharding import PartitionSpec as P

BF16 = jnp.bfloat16
F32 = jnp.float32


def exchange(x, axis):
    return lax.all_to_all(x, axis, split_axis=0, concat_axis=0, tiled=True)


def gather(x, axis):
    n = lax.axis_size(axis)
    return exchange(jnp.broadcast_to(x[None], (n,) + x.shape), axis)


def per_device(inputs, out_grad, first_factor, second_factor, gate_weight):
    nd = lax.axis_size("dp")
    ns = lax.axis_size("seq")
    _, rows, width = inputs.shape
    blocks, part, length = first_factor.shape
    cols, part2, size2 = second_factor.shape
    crows, cpart = gate_weight.shape
    flat = inputs.reshape(rows, width)
    blocked = inputs.reshape(blocks, length, width)
    cot = out_grad.reshape(rows, width).astype(F32)

    first = gather(first_factor, "dp").transpose(1, 0, 2, 3).reshape(blocks, length, length)
    one = jnp.einsum("bjk,bkd->bjd", first, blocked, preferred_element_type=F32).astype(BF16)
    one = one.reshape(blocks, ns, cols, width).transpose(1, 0, 2, 3)
    col_one = exchange(one, "seq").reshape(size2, cols, width)

    gate_full = gather(gate_weight, "seq").reshape(width, cpart)
    gate_full = gather(gate_full, "dp").transpose(1, 0, 2).reshape(width, width)
    second = gather(second_factor, "dp").transpose(1, 0, 2, 3).reshape(cols, size2, size2)

    gate = jax.nn.sigmoid(jnp.dot(flat, gate_full, preferred_element_type=F32))
    mgrad = (cot * gate).astype(BF16)
    mgrad = mgrad.reshape(blocks, ns, cols, width).transpose(1, 0, 2, 3)

    col_two = jnp.einsum("jpq,qjd->pjd", second, col_one, preferred_element_type=F32).astype(BF16)
    col_two = col_two.reshape(ns, blocks, cols, width)
    both = exchange(jnp.concatenate([mgrad, col_two], axis=1), "seq")
    col_grad = both[:, :blocks].reshape(size2, cols, width)
    two = both[:, blocks:].transpose(1, 0, 2, 3).reshape(rows, width)

    col_back = jnp.einsum("jpq,pjd->qjd", second, col_grad, preferred_element_type=F32).astype(BF16)
    back = exchange(col_back.reshape(ns, blocks, cols, width), "seq")
    back = back.transpose(1, 0, 2, 3).reshape(blocks, length, width)

    delta = (cot * two.astype(F32) * gate * (1.0 - gate)).astype(BF16)
    gpart = jnp.dot(flat.T, delta, preferred_element_type=F32)
    gpart = gpart.reshape(width, nd, cpart).transpose(1, 0, 2)
    gsum = exchange(gpart, "dp").sum(0)
    grad_gate = exchange(gsum.reshape(ns, crows, cpart), "seq").sum(0)

    spart = jnp.einsum("pjd,qjd->jpq", col_grad, col_one, preferred_element_type=F32)
    spart = spart.reshape(cols, nd, part2, size2).transpose(1, 0, 2, 3)
    grad_second = exchange(spart, "dp").sum(0)

    gate_input = jnp.dot(delta, gate_full.T, preferred_element_type=F32).astype(BF16)

    fpart = jnp.einsum("bjd,bkd->bjk", back, blocked, preferred_element_type=F32).astype(BF16)
    fpart = fpart.reshape(blocks, nd, part, length).transpose(1, 0, 2, 3)
    grad_first = exchange(fpart, "dp").astype(F32).sum(0)
    through = jnp.einsum("bjk,bjd->bkd", first, back, preferred_element_type=F32)
    grad_inputs = (through + gate_input.reshape(through.shape).astype(F32)).astype(BF16)
    return (grad_inputs.reshape(inputs.shape), grad_first, grad_second, grad_gate)


def solution(mesh):
    specs = (P("seq", "dp", None), P("seq", "dp", None), P("seq", "dp"))
    return jax.shard_map(
        per_device,
        mesh=mesh,
        in_specs=(P("dp", "seq", None), P("dp", "seq", None)) + specs,
        out_specs=(P("dp", "seq", None),) + specs,
        check_vma=False,
    )
```

```python
import jax
import jax.numpy as jnp
from jax import lax
from jax.sharding import Mesh, PartitionSpec as P

BF16 = jnp.bfloat16
F32 = jnp.float32
SEQ = ("z", "xh", "co")
DP = ("y", "xl")


def exchange(x, axis):
    return lax.all_to_all(x, axis, split_axis=0, concat_axis=0, tiled=True)


def spread(x, axis):
    n = lax.axis_size(axis)
    return exchange(jnp.broadcast_to(x[None], (n,) + x.shape), axis)


def gather(x, axes):
    out = x[None]
    for axis in reversed(axes):
        out = lax.all_gather(out, axis, axis=0, tiled=True)
    return out


def halve(x, axis, bit):
    n = lax.axis_size(axis)
    low = lax.axis_index(axis) & bit == 0
    keep = jnp.where(low, x[0], x[1])
    give = jnp.where(low, x[1], x[0])
    return keep + lax.ppermute(give, axis, [(i, i ^ bit) for i in range(n)])


def per_device(inputs, out_grad, first_factor, second_factor, gate_weight):
    nd = lax.axis_size(DP)
    ns = lax.axis_size(SEQ)
    nz = lax.axis_size("z")
    _, rows, width = inputs.shape
    blocks, part, length = first_factor.shape
    cols, part2, size2 = second_factor.shape
    crows, cpart = gate_weight.shape
    flat = inputs.reshape(rows, width)
    blocked = inputs.reshape(blocks, length, width)
    cot = out_grad.reshape(rows, width).astype(F32)

    first = spread(first_factor, DP).transpose(1, 0, 2, 3).reshape(blocks, length, length)
    second = gather(second_factor, DP).transpose(1, 0, 2, 3).reshape(cols, size2, size2)
    gate_full = gather(gate_weight, SEQ).reshape(width, cpart)
    gate_full = gather(gate_full, DP).transpose(1, 0, 2).reshape(width, width)

    one = jnp.einsum("bjk,bkd->bjd", first, blocked, preferred_element_type=F32).astype(BF16)
    one = one.reshape(blocks, ns, cols, width).transpose(1, 0, 2, 3)
    col_one = exchange(one, SEQ).reshape(size2, cols, width)

    gate = jax.nn.sigmoid(jnp.dot(flat, gate_full, preferred_element_type=F32))
    mgrad = (cot * gate).astype(BF16)
    mgrad = mgrad.reshape(blocks, ns, cols, width).transpose(1, 0, 2, 3)

    col_two = jnp.einsum("jpq,qjd->pjd", second, col_one, preferred_element_type=F32).astype(BF16)
    col_two = col_two.reshape(ns, blocks, cols, width)
    both = exchange(jnp.concatenate([mgrad, col_two], axis=1), SEQ)
    col_grad = both[:, :blocks].reshape(size2, cols, width)
    two = both[:, blocks:].transpose(1, 0, 2, 3).reshape(rows, width)

    col_back = jnp.einsum("jpq,pjd->qjd", second, col_grad, preferred_element_type=F32).astype(BF16)
    spart = jnp.einsum("pjd,qjd->jpq", col_grad, col_one, preferred_element_type=F32)
    two, col_back, spart = lax.optimization_barrier((two, col_back, spart))
    back = exchange(col_back.reshape(ns, blocks, cols, width), SEQ)
    back = back.transpose(1, 0, 2, 3).reshape(blocks, length, width)
    grad_second = lax.psum_scatter(spart, DP, scatter_dimension=1, tiled=True)

    delta = (cot * two.astype(F32) * gate * (1.0 - gate)).astype(BF16)
    gpart = jnp.dot(delta.T, flat, preferred_element_type=F32)
    gsum = gpart.reshape(lax.axis_size("y"), 2, cpart, width)
    gsum = halve(gsum.transpose(1, 0, 2, 3), "xl", 1)
    gsum = halve(gsum.reshape(2, 2, cpart, width), "y", 2)
    gsum = halve(gsum, "y", 1)
    gsum = gsum.T.reshape(ns // 2, 2, crows, cpart).transpose(1, 0, 2, 3)
    gsum = halve(gsum, "co", 1)
    gsum = halve(gsum.reshape(nz, 2, crows, cpart).transpose(1, 0, 2, 3), "xh", 1)
    while nz > 1:
        nz //= 2
        gsum = halve(gsum.reshape(2, nz, crows, cpart), "z", nz)
    grad_gate = gsum.reshape(crows, cpart)

    gate_input = jnp.dot(delta, gate_full.T, preferred_element_type=F32).astype(BF16)

    fpart = jnp.einsum("bjd,bkd->bjk", back, blocked, preferred_element_type=F32).astype(BF16)
    fpart = fpart.reshape(blocks, nd, part, length).transpose(1, 0, 2, 3)
    grad_first = exchange(fpart, DP).astype(F32).sum(0)
    through = jnp.einsum("bjk,bjd->bkd", first, back, preferred_element_type=F32)
    grad_inputs = (through + gate_input.reshape(through.shape).astype(F32)).astype(BF16)
    return (grad_inputs.reshape(inputs.shape), grad_first, grad_second, grad_gate)


def solution(mesh):
    fine = Mesh(mesh.devices.reshape(16, 2, 2, 4, 2), SEQ + DP)
    specs = (P(SEQ, DP, None), P(SEQ, DP, None), P(SEQ, DP))
    return jax.shard_map(
        per_device,
        mesh=fine,
        in_specs=(P(DP, SEQ, None), P(DP, SEQ, None)) + specs,
        out_specs=(P(DP, SEQ, None),) + specs,
        check_vma=False,
    )
```

```python
import functools

import jax
import jax.numpy as jnp
from jax import lax
from jax.experimental import pallas as pl
from jax.experimental.pallas import tpu as pltpu
from jax.sharding import Mesh, PartitionSpec as P

BF16 = jnp.bfloat16
F32 = jnp.float32
SEQ = ("z", "xh", "co")
DP = ("y", "xl")
VMEM = pl.BlockSpec(memory_space=pltpu.VMEM)
SMEM = pl.BlockSpec(memory_space=pltpu.SMEM)


def exchange(x, axis):
    return lax.all_to_all(x, axis, split_axis=0, concat_axis=0, tiled=True)


def spread(x, axis):
    n = lax.axis_size(axis)
    return exchange(jnp.broadcast_to(x[None], (n,) + x.shape), axis)


def gather(x, axes):
    out = x[None]
    for axis in reversed(axes):
        out = lax.all_gather(out, axis, axis=0, tiled=True)
    return out


def swap(x, axis, bits):
    n = lax.axis_size(axis)
    return lax.ppermute(x, axis, [(i, i ^ bits) for i in range(n)])


def local(body, out_shape, operands, in_specs=None, flops=0, scratch=()):
    outs = jax.tree.leaves(out_shape)
    moved = sum(a.size * a.dtype.itemsize for a in list(operands) + outs)
    return pl.pallas_call(
        body,
        grid=(1,),
        out_shape=out_shape,
        in_specs=in_specs or [VMEM] * len(operands),
        out_specs=jax.tree.map(lambda _: VMEM, out_shape),
        scratch_shapes=list(scratch),
        cost_estimate=pl.CostEstimate(flops=flops, bytes_accessed=moved, transcendentals=0),
        compiler_params=pltpu.CompilerParams(vmem_limit_bytes=40 << 20),
    )(*operands)


def shape(dims, dtype):
    return jax.ShapeDtypeStruct(dims, dtype)


def order_kernel(me_ref, *refs):
    out_ref = refs[-1]
    for far, ref in enumerate(refs[:-1]):
        for near in range(ref.shape[0]):
            out_ref[me_ref[0] ^ (far * ref.shape[0] + near)] = ref[near]


def gather_near(x, axis):
    n = lax.axis_size(axis)
    near = jnp.stack([x] + [swap(x, axis, k) for k in range(1, 4)])
    parts = [near] + [swap(near, axis, k) for k in range(4, n, 4)]
    return local(
        order_kernel,
        shape((n,) + x.shape, x.dtype),
        [lax.axis_index(axis)[None]] + parts,
        [SMEM] + [VMEM] * len(parts),
    )


def halve(x, axis, bit):
    low = lax.axis_index(axis) & bit == 0
    keep = jnp.where(low, x[0], x[1])
    give = jnp.where(low, x[1], x[0])
    return keep + swap(give, axis, bit)


def dot(a, b, ca=1, cb=0):
    return lax.dot_general(a, b, (((ca,), (cb,)), ((), ())), preferred_element_type=F32)


STEP = 32


def pack(tops, cols):
    return jnp.concatenate([t.reshape(-1, cols, t.shape[-1]) for t in tops], axis=1)


def rows_kernel(cols, first_ref, x_ref, out_ref):
    _, blocks, part, length = first_ref.shape
    per = STEP * cols // part
    for c in range(out_ref.shape[0] // STEP):
        tops = [
            dot(first_ref[c * per : (c + 1) * per, b].reshape(per * part, length), x_ref[b])
            for b in range(blocks)
        ]
        out_ref[c * STEP : (c + 1) * STEP] = pack(tops, cols).astype(BF16)


def gate_kernel(cols, x_ref, weight_ref, cot_ref, out_ref, slope_ref):
    blocks = x_ref.shape[0]
    for c in range(out_ref.shape[0] // STEP):
        rows = pl.ds(c * STEP * cols, STEP * cols)
        tops = []
        for b in range(blocks):
            gate = jax.nn.sigmoid(dot(x_ref[b, rows], weight_ref[...]))
            grad = cot_ref[b, rows].astype(F32) * gate
            slope_ref[b, rows] = grad * (1.0 - gate)
            tops.append(grad)
        out_ref[c * STEP : (c + 1) * STEP] = pack(tops, cols).astype(BF16)


LANES = 128


def unfold(src_ref, tmp_ref):
    tall = src_ref.shape[1]
    for c in range(0, src_ref.shape[0], STEP):
        piece = src_ref[c : c + STEP].astype(F32).reshape(STEP * tall, src_ref.shape[2])
        for k in range(tmp_ref.shape[0]):
            tmp_ref[k, pl.ds(c * tall, STEP * tall)] = piece[:, k * LANES : (k + 1) * LANES]


def fold(tmp_ref, dst_ref, first):
    tall = tmp_ref.shape[1] // dst_ref.shape[0]
    for c in range(0, dst_ref.shape[0], STEP):
        for k in range(tmp_ref.shape[0]):
            piece = tmp_ref[k, pl.ds(c * tall, STEP * tall)].reshape(STEP, tall, LANES)
            dst_ref[c : c + STEP, first : first + tall, k * LANES : (k + 1) * LANES] = piece.astype(BF16)


def column(tmp_ref, j, cols):
    rows = pl.ds(j, tmp_ref.shape[1] // cols, stride=cols)
    return jnp.concatenate([tmp_ref[k, rows] for k in range(tmp_ref.shape[0])], axis=1)


def set_column(tmp_ref, j, cols, value):
    rows = pl.ds(j, tmp_ref.shape[1] // cols, stride=cols)
    for k in range(tmp_ref.shape[0]):
        tmp_ref[k, rows] = value[:, k * LANES : (k + 1) * LANES]


def forward_kernel(second_ref, one_ref, grad_ref, both_ref, by_ref, tmp_ref, res_ref):
    _, cols, _, size = second_ref.shape
    rows = grad_ref.shape[1]
    for c in range(0, grad_ref.shape[0], STEP):
        both_ref[c : c + STEP, :rows] = grad_ref[c : c + STEP]
    unfold(one_ref, tmp_ref)
    for j in range(cols):
        mine = column(tmp_ref, j, cols).astype(BF16)
        by_ref[j] = mine
        set_column(res_ref, j, cols, dot(second_ref[:, j].reshape(size, size), mine))
    fold(res_ref, both_ref, rows)


def backward_kernel(second_ref, both_ref, by_ref, back_ref, part_ref, tmp_ref, res_ref):
    nd, cols, part, size = second_ref.shape
    unfold(both_ref, tmp_ref)
    for j in range(cols):
        mine = column(tmp_ref, j, cols).astype(BF16)
        weight = second_ref[:, j].reshape(size, size)
        set_column(res_ref, j, cols, dot(weight, mine, 0, 0))
        part_ref[j] = dot(mine, by_ref[j], 1, 1)
    fold(res_ref, back_ref, 0)


def delta_kernel(cols, both_ref, slope_ref, x_ref, weight_ref, input_ref, part_ref, delta_ref):
    blocks, length, _ = x_ref.shape
    n = STEP * cols
    for c in range(both_ref.shape[0] // STEP):
        two = both_ref[c * STEP : (c + 1) * STEP].astype(F32)
        for b in range(blocks):
            rows = pl.ds(c * n, n)
            mine = two[:, b * cols : (b + 1) * cols].reshape(n, two.shape[2])
            delta_ref[b, rows] = (mine * slope_ref[b, rows]).astype(BF16)
    for b in range(blocks):
        add = dot(delta_ref[b], x_ref[b], 0, 0)
        part_ref[...] = add if b == 0 else part_ref[...] + add
        input_ref[b] = dot(delta_ref[b], weight_ref[...], 1, 1).astype(BF16)


def unpack(src_ref, cols, b):
    piece = src_ref[...].astype(F32)[:, b * cols : (b + 1) * cols]
    return piece.reshape(-1, piece.shape[2]).astype(BF16)


def outer_kernel(cols, back_ref, x_ref, part_ref, by_ref):
    nd, blocks, part, length = part_ref.shape
    for b in range(blocks):
        by_ref[b] = unpack(back_ref, cols, b)
        part_ref[:, b] = dot(by_ref[b], x_ref[b], 1, 1).astype(BF16).reshape(nd, part, length)


def inputs_kernel(first_ref, by_ref, input_ref, out_ref):
    nd, blocks, part, length = first_ref.shape
    for b in range(blocks):
        through = dot(first_ref[:, b].reshape(nd * part, length), by_ref[b], 0, 0)
        out_ref[b] = (through + input_ref[b].astype(F32)).astype(BF16)


def per_device(inputs, out_grad, first_factor, second_factor, gate_weight):
    nd = lax.axis_size(DP)
    ns = lax.axis_size(SEQ)
    nz = lax.axis_size("z")
    _, rows, width = inputs.shape
    blocks, part, length = first_factor.shape
    cols, part2, size2 = second_factor.shape
    crows, cpart = gate_weight.shape
    x = inputs.reshape(blocks, length, width)
    cot = out_grad.reshape(blocks, length, width)
    tall = blocks * cols
    wide = 2 * rows * width * width
    cells = pltpu.VMEM((width // LANES, ns * tall, LANES), F32)

    first = spread(first_factor, DP)
    gate_part = gather_near(gate_weight, "z")
    one = local(
        functools.partial(rows_kernel, cols), shape((ns, tall, width), BF16), [first, x], flops=wide
    )
    one, gate_part, second_factor = lax.optimization_barrier((one, gate_part, second_factor))
    gate_part = gather(gate_part, SEQ[1:]).transpose(1, 0, 2, 3).reshape(width, cpart)
    second = gather(second_factor, DP)
    gate_full = gather(gate_part, DP).transpose(1, 0, 2).reshape(width, width)

    mixed_grad, slope = local(
        functools.partial(gate_kernel, cols),
        (shape((ns, tall, width), BF16), shape(x.shape, F32)),
        [x, gate_full, cot],
        flops=wide,
    )
    col_one = exchange(one, SEQ)
    both, by_col = local(
        forward_kernel,
        (shape((ns, 2 * tall, width), BF16), shape((cols, size2, width), BF16)),
        [second, col_one, mixed_grad],
        flops=wide // 4,
        scratch=[cells, cells],
    )
    both = exchange(both, SEQ)
    half = [
        pl.BlockSpec((ns, tall, width), functools.partial(lambda k, i: (0, k, 0), k))
        for k in range(2)
    ]
    col_back, spart = local(
        backward_kernel,
        (shape((ns, tall, width), BF16), shape((cols, size2, size2), F32)),
        [second, both, by_col],
        [VMEM, half[0], VMEM],
        flops=wide // 2,
        scratch=[cells, cells],
    )
    both, col_back, spart = lax.optimization_barrier((both, col_back, spart))
    back = exchange(col_back, SEQ)
    grad_second = lax.psum_scatter(spart, DP, scatter_dimension=1, tiled=True)

    gate_input, gsum = local(
        functools.partial(delta_kernel, cols),
        (shape(x.shape, BF16), shape((width, width), F32)),
        [both, slope, x, gate_full],
        [half[1], VMEM, VMEM, VMEM],
        flops=2 * wide,
        scratch=[pltpu.VMEM(x.shape, BF16)],
    )
    gsum = gsum.reshape(lax.axis_size("y"), 2, cpart, width)
    gsum = halve(gsum.transpose(1, 0, 2, 3), "xl", 1)
    gsum = halve(gsum.reshape(2, 2, cpart, width), "y", 2)
    gsum = halve(gsum, "y", 1)
    gsum, grad_second = lax.optimization_barrier((gsum, grad_second))
    gsum = gsum.T.reshape(ns // 2, 2, crows, cpart).transpose(1, 0, 2, 3)
    gsum = halve(gsum, "co", 1)
    gsum = halve(gsum.reshape(nz, 2, crows, cpart).transpose(1, 0, 2, 3), "xh", 1)
    fpart, by_row = local(
        functools.partial(outer_kernel, cols),
        (shape(first.shape, BF16), shape(x.shape, BF16)),
        [back, x],
        flops=wide,
    )
    gsum, fpart = lax.optimization_barrier((gsum, fpart))
    while nz > 1:
        nz //= 2
        gsum = halve(gsum.reshape(2, nz, crows, cpart), "z", nz)
    grad_gate = gsum.reshape(crows, cpart)
    grad_first = exchange(fpart, DP).astype(F32).sum(0)
    grad_inputs = local(inputs_kernel, shape(x.shape, BF16), [first, by_row, gate_input], flops=wide)
    return (grad_inputs.reshape(inputs.shape), grad_first, grad_second, grad_gate)


def solution(mesh):
    fine = Mesh(mesh.devices.reshape(16, 2, 2, 4, 2), SEQ + DP)
    specs = (P(SEQ, DP, None), P(SEQ, DP, None), P(SEQ, DP))
    return jax.shard_map(
        per_device,
        mesh=fine,
        in_specs=(P(DP, SEQ, None), P(DP, SEQ, None)) + specs,
        out_specs=(P(DP, SEQ, None),) + specs,
        check_vma=False,
    )
```

```python
import functools

import jax
import jax.numpy as jnp
from jax import lax
from jax.experimental import pallas as pl
from jax.experimental.pallas import tpu as pltpu
from jax.sharding import Mesh, PartitionSpec as P

BF16 = jnp.bfloat16
F32 = jnp.float32
SEQ = ("z", "xh", "co")
DP = ("y", "xl")
VMEM = pl.BlockSpec(memory_space=pltpu.VMEM)
ANY = pl.BlockSpec(memory_space=pl.ANY)
SMEM = pl.BlockSpec(memory_space=pltpu.SMEM)


def exchange(x, axis):
    return lax.all_to_all(x, axis, split_axis=0, concat_axis=0, tiled=True)


def gather(x, axes):
    out = x[None]
    for axis in reversed(axes):
        out = lax.all_gather(out, axis, axis=0, tiled=True)
    return out


def swap(x, axis, bits):
    n = lax.axis_size(axis)
    return lax.ppermute(x, axis, [(i, i ^ bits) for i in range(n)])


def local(body, out_shape, operands, in_specs=None, flops=0, scratch=()):
    outs = jax.tree.leaves(out_shape)
    moved = sum(a.size * a.dtype.itemsize for a in list(operands) + outs)
    return pl.pallas_call(
        body,
        grid=(1,),
        out_shape=out_shape,
        in_specs=in_specs or [VMEM] * len(operands),
        out_specs=jax.tree.map(lambda _: VMEM, out_shape),
        scratch_shapes=list(scratch),
        cost_estimate=pl.CostEstimate(flops=flops, bytes_accessed=moved, transcendentals=0),
        compiler_params=pltpu.CompilerParams(vmem_limit_bytes=28 << 20),
    )(*operands)


def shape(dims, dtype):
    return jax.ShapeDtypeStruct(dims, dtype)


def order_kernel(me_ref, low_ref, high_ref, after_ref, out_ref):
    del after_ref
    n = low_ref.shape[0]
    for k in range(n):
        out_ref[me_ref[0] ^ k] = low_ref[k]
        out_ref[me_ref[0] ^ (n + k)] = high_ref[k]


def double(x, axis):
    low, bit = x[None], 1
    while True:
        high = swap(low, axis, bit)
        bit *= 2
        if bit == lax.axis_size(axis):
            return low, high
        low = jnp.concatenate([low, high])


def halve(x, axis, bit):
    low = lax.axis_index(axis) & bit == 0
    keep = jnp.where(low, x[0], x[1])
    give = jnp.where(low, x[1], x[0])
    return keep, swap(give, axis, bit)


def dot(a, b, ca=1, cb=0):
    return lax.dot_general(a, b, (((ca,), (cb,)), ((), ())), preferred_element_type=F32)


STEP = 32
LANES = 128


def pack(tops, cols):
    return jnp.concatenate([t.reshape(-1, cols, t.shape[-1]) for t in tops], axis=1)


def beside(j, part, width):
    per = width // LANES
    return pl.ds((j // per) * part, part), pl.ds((j % per) * LANES, LANES)


def weights_kernel(first_ref, second_ref, out_ref):
    blocks, part, width = first_ref.shape
    for d in range(out_ref.shape[0]):
        for b in range(blocks):
            out_ref[d, b * part : (b + 1) * part] = first_ref[b]
        for j in range(second_ref.shape[0]):
            rows, lanes = beside(j, second_ref.shape[1], width)
            out_ref[d, pl.ds(blocks * part + rows.start, rows.size), lanes] = second_ref[j]


def second_of(second_ref, j):
    nd, _, width = second_ref.shape
    rows, lanes = beside(j, LANES // nd, width)
    return second_ref[:, rows, lanes].reshape(LANES, LANES)


def rows_kernel(cols, weights_ref, x_ref, out_ref):
    nd, (blocks, length, _) = weights_ref.shape[0], x_ref.shape
    part = length // nd
    per = STEP * cols // part
    for c in range(out_ref.shape[0] // STEP):
        tops = []
        for b in range(blocks):
            mine = weights_ref[c * per : (c + 1) * per, b * part : (b + 1) * part]
            tops.append(dot(mine.reshape(per * part, length), x_ref[b]))
        out_ref[c * STEP : (c + 1) * STEP] = pack(tops, cols).astype(BF16)


def gate_kernel(cols, x_ref, weight_ref, cot_ref, out_ref, slope_ref):
    blocks = x_ref.shape[0]
    for c in range(out_ref.shape[0] // STEP):
        rows = pl.ds(c * STEP * cols, STEP * cols)
        tops = []
        for b in range(blocks):
            gate = jax.nn.sigmoid(dot(x_ref[b, rows], weight_ref[...]))
            grad = cot_ref[b, rows].astype(F32) * gate
            slope_ref[b, rows] = grad * (1.0 - gate)
            tops.append(grad)
        out_ref[c * STEP : (c + 1) * STEP] = pack(tops, cols).astype(BF16)


def unfold(src_ref, tmp_ref):
    tall = src_ref.shape[1]
    for c in range(0, src_ref.shape[0], STEP):
        piece = src_ref[c : c + STEP].astype(F32).reshape(STEP * tall, src_ref.shape[2])
        for k in range(tmp_ref.shape[0]):
            tmp_ref[k, pl.ds(c * tall, STEP * tall)] = piece[:, k * LANES : (k + 1) * LANES]


def fold(tmp_ref, dst_ref):
    tall = dst_ref.shape[1]
    for c in range(0, dst_ref.shape[0], STEP):
        rows = pl.ds(c * tall, STEP * tall)
        piece = jnp.concatenate([tmp_ref[k, rows] for k in range(tmp_ref.shape[0])], axis=1)
        dst_ref[c : c + STEP] = piece.reshape(STEP, tall, dst_ref.shape[2]).astype(BF16)


def column(tmp_ref, j, cols):
    rows = pl.ds(j, tmp_ref.shape[1] // cols, stride=cols)
    return jnp.concatenate([tmp_ref[k, rows] for k in range(tmp_ref.shape[0])], axis=1)


def set_column(tmp_ref, j, cols, value):
    rows = pl.ds(j, tmp_ref.shape[1] // cols, stride=cols)
    for k in range(tmp_ref.shape[0]):
        tmp_ref[k, rows] = value[:, k * LANES : (k + 1) * LANES]


def forward_kernel(second_ref, one_ref, two_ref, by_ref, tmp_ref, res_ref):
    unfold(one_ref, tmp_ref)
    cols = by_ref.shape[0]
    for j in range(cols):
        mine = column(tmp_ref, j, cols).astype(BF16)
        by_ref[j] = mine
        set_column(res_ref, j, cols, dot(second_of(second_ref, j), mine))
    fold(res_ref, two_ref)


def backward_kernel(second_ref, grad_ref, by_ref, back_ref, part_ref, tmp_ref, res_ref):
    unfold(grad_ref, tmp_ref)
    cols = by_ref.shape[0]
    nd, _, width = part_ref.shape
    for j in range(cols):
        mine = column(tmp_ref, j, cols).astype(BF16)
        set_column(res_ref, j, cols, dot(second_of(second_ref, j), mine, 0, 0))
        rows, lanes = beside(j, LANES // nd, width)
        part = dot(mine, by_ref[j], 1, 1).reshape(nd, LANES // nd, LANES)
        part_ref[:, rows, lanes] = part.astype(BF16)
    fold(res_ref, back_ref)


def delta_kernel(
    cols, me_ref, two_ref, slope_ref, x_ref, weight_ref, input_ref, keep_ref, give_ref, delta_ref, sum_ref
):
    blocks, length, _ = x_ref.shape
    n = STEP * cols
    for c in range(two_ref.shape[0] // STEP):
        two = two_ref[c * STEP : (c + 1) * STEP].astype(F32)
        for b in range(blocks):
            rows = pl.ds(c * n, n)
            mine = two[:, b * cols : (b + 1) * cols].reshape(n, two.shape[2])
            delta_ref[b, rows] = (mine * slope_ref[b, rows]).astype(BF16)
    pairs, cpart, width = keep_ref.shape
    for b in range(blocks):
        add = dot(delta_ref[b], x_ref[b], 0, 0).reshape(pairs, 2, cpart, width)
        for k in range(2):
            sum_ref[k] = add[:, k] if b == 0 else sum_ref[k] + add[:, k]
        input_ref[b] = dot(delta_ref[b], weight_ref[...], 1, 1).astype(BF16)
    keep_ref[...] = sum_ref[me_ref[0]]
    give_ref[...] = sum_ref[1 - me_ref[0]].astype(BF16)


def turn_kernel(keep_ref, got_ref, after_ref, out_ref):
    del after_ref
    near, far, nz, crows, cpart = out_ref.shape
    whole = (keep_ref[...] + got_ref[...]).T.reshape(nz, far, near, crows, cpart)
    for k in range(near):
        for h in range(far):
            out_ref[k, h] = whole[:, h, k]


def outer_kernel(cols, back_ref, x_ref, second_ref, part_ref, by_ref):
    blocks, length, _ = x_ref.shape
    nd, rows, width = part_ref.shape
    part = length // nd
    for b in range(blocks):
        piece = back_ref[...].astype(F32)[:, b * cols : (b + 1) * cols]
        by_ref[b] = piece.reshape(length, width).astype(BF16)
        add = dot(by_ref[b], x_ref[b], 1, 1).astype(BF16)
        part_ref[:, b * part : (b + 1) * part] = add.reshape(nd, part, width)
    part_ref[:, blocks * part :] = second_ref[...]


def inputs_kernel(weights_ref, by_ref, input_ref, out_ref):
    nd, (blocks, length, _) = weights_ref.shape[0], by_ref.shape
    part = length // nd
    for b in range(blocks):
        mine = weights_ref[:, b * part : (b + 1) * part].reshape(length, length)
        through = dot(mine, by_ref[b], 0, 0)
        out_ref[b] = (through + input_ref[b].astype(F32)).astype(BF16)


def total_kernel(parts_ref, first_ref, second_ref):
    nd, _, width = parts_ref.shape
    blocks, part, _ = first_ref.shape
    for b in range(blocks):
        rows = pl.ds(b * part, part)
        first_ref[b] = sum(parts_ref[d, rows].astype(F32) for d in range(nd))
    for j in range(second_ref.shape[0]):
        rows, lanes = beside(j, second_ref.shape[1], width)
        rows = pl.ds(blocks * part + rows.start, rows.size)
        second_ref[j] = sum(parts_ref[d, rows, lanes].astype(F32) for d in range(nd))


def per_device(inputs, out_grad, first_factor, second_factor, gate_weight):
    nd = lax.axis_size(DP)
    ns = lax.axis_size(SEQ)
    ny = lax.axis_size("y")
    nz = lax.axis_size("z")
    _, rows, width = inputs.shape
    blocks, part, length = first_factor.shape
    cols, part2, size2 = second_factor.shape
    crows, cpart = gate_weight.shape
    x = inputs.reshape(blocks, length, width)
    cot = out_grad.reshape(blocks, length, width)
    piece = shape((ns, blocks * cols, width), BF16)
    wide = 2 * rows * width * width
    cells = pltpu.VMEM((width // LANES, rows, LANES), F32)
    tail = cols * part2 * size2 // width
    both_rows = blocks * part + tail
    by_second = pl.BlockSpec((nd, tail, width), lambda i: (0, blocks * part // tail, 0))

    weights = local(
        weights_kernel, shape((nd, both_rows, width), BF16), [first_factor, second_factor]
    )
    weights = exchange(weights, DP)
    one = local(functools.partial(rows_kernel, cols), piece, [weights, x], flops=wide)
    one, gate_weight = lax.optimization_barrier((one, gate_weight))
    gate_low, gate_high = double(gate_weight, "z")
    col_one = exchange(one, SEQ)
    col_one, gate_low, gate_high = lax.optimization_barrier((col_one, gate_low, gate_high))
    col_two, by_col = local(
        forward_kernel,
        (piece, shape((cols, size2, width), BF16)),
        [weights, col_one],
        [by_second, VMEM],
        flops=wide // 4,
        scratch=[cells, cells],
    )
    two = exchange(col_two, SEQ)

    gate_part = local(
        order_kernel,
        shape((nz, crows, cpart), BF16),
        [lax.axis_index("z")[None], gate_low, gate_high, col_two],
        [SMEM, VMEM, VMEM, ANY],
    )
    gate_part = gather(gate_part, SEQ[1:]).transpose(1, 0, 2, 3).reshape(width, cpart)
    gate_full = gather(gate_part, DP).transpose(1, 0, 2).reshape(width, width)
    mixed_grad, slope = local(
        functools.partial(gate_kernel, cols),
        (piece, shape(x.shape, F32)),
        [x, gate_full, cot],
        flops=wide,
    )
    two, mixed_grad = lax.optimization_barrier((two, mixed_grad))
    col_grad = exchange(mixed_grad, SEQ)

    gate_input, keep, give = local(
        functools.partial(delta_kernel, cols),
        (
            shape(x.shape, BF16),
            shape((ny, cpart, width), F32),
            shape((ny, cpart, width), BF16),
        ),
        [lax.axis_index("xl")[None], two, slope, x, gate_full],
        [SMEM] + [VMEM] * 4,
        flops=2 * wide,
        scratch=[pltpu.VMEM(x.shape, BF16), pltpu.VMEM((2, ny, cpart, width), F32)],
    )
    gsum = keep + swap(give, "xl", 1).astype(F32)
    keep, got = halve(gsum.reshape(2, ny // 2, cpart, width), "y", 2)
    keep, got = halve(keep + got, "y", 1)
    col_grad, keep, got = lax.optimization_barrier((col_grad, keep, got))

    col_back, spart = local(
        backward_kernel,
        (piece, shape((nd, tail, width), BF16)),
        [weights, col_grad, by_col],
        [by_second, VMEM, VMEM],
        flops=wide // 2,
        scratch=[cells, cells],
    )
    back = exchange(col_back, SEQ)
    gsum = local(
        turn_kernel,
        shape((2, 2, nz, crows, cpart), F32),
        [keep, got, col_back],
        [VMEM, VMEM, ANY],
    )
    keep, got = halve(gsum, "co", 1)
    keep, got = halve(keep + got, "xh", 1)
    bit = nz
    while bit > 4:
        bit //= 2
        keep, got = halve((keep + got).reshape(2, bit, crows, cpart), "z", bit)

    parts, by_row = local(
        functools.partial(outer_kernel, cols),
        (shape(weights.shape, BF16), shape(x.shape, BF16)),
        [back, x, spart],
        flops=wide,
    )
    keep, got, parts = lax.optimization_barrier((keep, got, parts))
    parts = exchange(parts, DP)
    while bit > 1:
        bit //= 2
        keep, got = halve((keep + got).reshape(2, bit, crows, cpart), "z", bit)
    grad_gate = (keep + got).reshape(crows, cpart)
    grad_inputs = local(inputs_kernel, shape(x.shape, BF16), [weights, by_row, gate_input], flops=wide)
    grad_first, grad_second = local(
        total_kernel, (shape(first_factor.shape, F32), shape(second_factor.shape, F32)), [parts]
    )
    return (grad_inputs.reshape(inputs.shape), grad_first, grad_second, grad_gate)


def solution(mesh):
    fine = Mesh(mesh.devices.reshape(16, 2, 2, 4, 2), SEQ + DP)
    specs = (P(SEQ, DP, None), P(SEQ, DP, None), P(SEQ, DP))
    return jax.shard_map(
        per_device,
        mesh=fine,
        in_specs=(P(DP, SEQ, None), P(DP, SEQ, None)) + specs,
        out_specs=(P(DP, SEQ, None),) + specs,
        check_vma=False,
    )
```

```python
import functools

import jax
import jax.numpy as jnp
from jax import lax
from jax.experimental import pallas as pl
from jax.experimental.pallas import tpu as pltpu
from jax.sharding import Mesh, PartitionSpec as P

BF16 = jnp.bfloat16
F32 = jnp.float32
SEQ = ("z", "xh", "co")
DP = ("y", "xl")
VMEM = pl.BlockSpec(memory_space=pltpu.VMEM)
ANY = pl.BlockSpec(memory_space=pl.ANY)
SMEM = pl.BlockSpec(memory_space=pltpu.SMEM)


def exchange(x, axis):
    return lax.all_to_all(x, axis, split_axis=0, concat_axis=0, tiled=True)


def gather(x, axes):
    out = x[None]
    for axis in reversed(axes):
        out = lax.all_gather(out, axis, axis=0, tiled=True)
    return out


def swap(x, axis, bits):
    n = lax.axis_size(axis)
    return lax.ppermute(x, axis, [(i, i ^ bits) for i in range(n)])


def local(body, out_shape, operands, in_specs=None, out_specs=None, flops=0, scratch=(), alias=None):
    outs = jax.tree.leaves(out_shape)
    moved = sum(a.size * a.dtype.itemsize for a in list(operands) + outs)
    return pl.pallas_call(
        body,
        grid=(1,),
        out_shape=out_shape,
        in_specs=in_specs or [VMEM] * len(operands),
        out_specs=out_specs or jax.tree.map(lambda _: VMEM, out_shape),
        input_output_aliases=alias or {},
        scratch_shapes=list(scratch),
        cost_estimate=pl.CostEstimate(flops=flops, bytes_accessed=moved, transcendentals=0),
        compiler_params=pltpu.CompilerParams(vmem_limit_bytes=28 << 20),
    )(*operands)


def shape(dims, dtype):
    return jax.ShapeDtypeStruct(dims, dtype)


def halve(x, axis, bit):
    low = lax.axis_index(axis) & bit == 0
    keep = jnp.where(low, x[0], x[1])
    give = jnp.where(low, x[1], x[0])
    return keep, swap(give, axis, bit)


def dot(a, b, ca=1, cb=0):
    return lax.dot_general(a, b, (((ca,), (cb,)), ((), ())), preferred_element_type=F32)


STEP = 32
LANES = 128


def pack(tops, cols):
    return jnp.concatenate([t.reshape(-1, cols, t.shape[-1]) for t in tops], axis=1)


def beside(j, part, width):
    per = width // LANES
    return pl.ds((j // per) * part, part), pl.ds((j % per) * LANES, LANES)


def weights_kernel(first_ref, second_ref, out_ref):
    blocks, part, width = first_ref.shape
    for d in range(out_ref.shape[0]):
        for b in range(blocks):
            out_ref[d, b * part : (b + 1) * part] = first_ref[b]
        for j in range(second_ref.shape[0]):
            rows, lanes = beside(j, second_ref.shape[1], width)
            out_ref[d, pl.ds(blocks * part + rows.start, rows.size), lanes] = second_ref[j]


def second_of(second_ref, j):
    nd, _, width = second_ref.shape
    rows, lanes = beside(j, LANES // nd, width)
    return second_ref[:, rows, lanes].reshape(LANES, LANES)


def rows_kernel(cols, weights_ref, x_ref, out_ref):
    nd, (blocks, length, _) = weights_ref.shape[0], x_ref.shape
    part = length // nd
    per = STEP * cols // part
    for c in range(out_ref.shape[0] // STEP):
        tops = []
        for b in range(blocks):
            mine = weights_ref[c * per : (c + 1) * per, b * part : (b + 1) * part]
            tops.append(dot(mine.reshape(per * part, length), x_ref[b]))
        out_ref[c * STEP : (c + 1) * STEP] = pack(tops, cols).astype(BF16)


def gate_kernel(cols, x_ref, weight_ref, cot_ref, out_ref, slope_ref):
    blocks = x_ref.shape[0]
    for c in range(out_ref.shape[0] // STEP):
        rows = pl.ds(c * STEP * cols, STEP * cols)
        tops = []
        for b in range(blocks):
            gate = jax.nn.sigmoid(dot(x_ref[b, rows], weight_ref[...]))
            grad = cot_ref[b, rows].astype(F32) * gate
            slope_ref[b, rows] = grad * (1.0 - gate)
            tops.append(grad)
        out_ref[c * STEP : (c + 1) * STEP] = pack(tops, cols).astype(BF16)


def unfold(src_ref, tmp_ref):
    tall = src_ref.shape[1]
    for c in range(0, src_ref.shape[0], STEP):
        piece = src_ref[c : c + STEP].astype(F32).reshape(STEP * tall, src_ref.shape[2])
        for k in range(tmp_ref.shape[0]):
            tmp_ref[k, pl.ds(c * tall, STEP * tall)] = piece[:, k * LANES : (k + 1) * LANES]


def fold(tmp_ref, dst_ref):
    tall = dst_ref.shape[1]
    for c in range(0, dst_ref.shape[0], STEP):
        rows = pl.ds(c * tall, STEP * tall)
        piece = jnp.concatenate([tmp_ref[k, rows] for k in range(tmp_ref.shape[0])], axis=1)
        dst_ref[c : c + STEP] = piece.reshape(STEP, tall, dst_ref.shape[2]).astype(BF16)


def column(tmp_ref, j, cols):
    rows = pl.ds(j, tmp_ref.shape[1] // cols, stride=cols)
    return jnp.concatenate([tmp_ref[k, rows] for k in range(tmp_ref.shape[0])], axis=1)


def set_column(tmp_ref, j, cols, value):
    rows = pl.ds(j, tmp_ref.shape[1] // cols, stride=cols)
    for k in range(tmp_ref.shape[0]):
        tmp_ref[k, rows] = value[:, k * LANES : (k + 1) * LANES]


def forward_kernel(second_ref, one_ref, grad_ref, two_ref, by_ref, tmp_ref, res_ref):
    del grad_ref
    unfold(one_ref, tmp_ref)
    cols = by_ref.shape[0]
    for j in range(cols):
        mine = column(tmp_ref, j, cols).astype(BF16)
        by_ref[j] = mine
        set_column(res_ref, j, cols, dot(second_of(second_ref, j), mine))
    fold(res_ref, two_ref)


def backward_kernel(second_ref, grad_ref, by_ref, back_ref, part_ref, tmp_ref, res_ref):
    unfold(grad_ref, tmp_ref)
    cols = by_ref.shape[0]
    nd, _, width = part_ref.shape
    for j in range(cols):
        mine = column(tmp_ref, j, cols).astype(BF16)
        set_column(res_ref, j, cols, dot(second_of(second_ref, j), mine, 0, 0))
        rows, lanes = beside(j, LANES // nd, width)
        part = dot(mine, by_ref[j], 1, 1).reshape(nd, LANES // nd, LANES)
        part_ref[:, rows, lanes] = part.astype(BF16)
    fold(res_ref, back_ref)


def delta_kernel(
    cols, me_ref, two_ref, slope_ref, x_ref, weight_ref, input_ref, keep_ref, give_ref, delta_ref, sum_ref
):
    blocks, length, _ = x_ref.shape
    n = STEP * cols
    for c in range(two_ref.shape[0] // STEP):
        two = two_ref[c * STEP : (c + 1) * STEP].astype(F32)
        for b in range(blocks):
            rows = pl.ds(c * n, n)
            mine = two[:, b * cols : (b + 1) * cols].reshape(n, two.shape[2])
            delta_ref[b, rows] = (mine * slope_ref[b, rows]).astype(BF16)
    pairs, cpart, width = keep_ref.shape
    for b in range(blocks):
        add = dot(delta_ref[b], x_ref[b], 0, 0).reshape(pairs, 2, cpart, width)
        for k in range(2):
            sum_ref[k] = add[:, k] if b == 0 else sum_ref[k] + add[:, k]
        input_ref[b] = dot(delta_ref[b], weight_ref[...], 1, 1).astype(BF16)
    keep_ref[...] = sum_ref[me_ref[0]]
    give_ref[...] = sum_ref[1 - me_ref[0]].astype(BF16)


def turn_kernel(keep_ref, got_ref, out_ref):
    near, far, nz, crows, cpart = out_ref.shape
    whole = (keep_ref[...] + got_ref[...]).T.reshape(nz, far, near, crows, cpart)
    for k in range(near):
        for h in range(far):
            out_ref[k, h] = whole[:, h, k]


def outer_kernel(cols, back_ref, x_ref, second_ref, part_ref, by_ref):
    blocks, length, _ = x_ref.shape
    nd, rows, width = part_ref.shape
    part = length // nd
    for b in range(blocks):
        piece = back_ref[...].astype(F32)[:, b * cols : (b + 1) * cols]
        by_ref[b] = piece.reshape(length, width).astype(BF16)
        add = dot(by_ref[b], x_ref[b], 1, 1).astype(BF16)
        part_ref[:, b * part : (b + 1) * part] = add.reshape(nd, part, width)
    part_ref[:, blocks * part :] = second_ref[...]


def inputs_kernel(weights_ref, by_ref, input_ref, out_ref):
    nd, (blocks, length, _) = weights_ref.shape[0], by_ref.shape
    part = length // nd
    for b in range(blocks):
        mine = weights_ref[:, b * part : (b + 1) * part].reshape(length, length)
        through = dot(mine, by_ref[b], 0, 0)
        out_ref[b] = (through + input_ref[b].astype(F32)).astype(BF16)


def total_kernel(parts_ref, first_ref, second_ref):
    nd, _, width = parts_ref.shape
    blocks, part, _ = first_ref.shape
    for b in range(blocks):
        rows = pl.ds(b * part, part)
        first_ref[b] = sum(parts_ref[d, rows].astype(F32) for d in range(nd))
    for j in range(second_ref.shape[0]):
        rows, lanes = beside(j, second_ref.shape[1], width)
        rows = pl.ds(blocks * part + rows.start, rows.size)
        second_ref[j] = sum(parts_ref[d, rows, lanes].astype(F32) for d in range(nd))


def per_device(inputs, out_grad, first_factor, second_factor, gate_weight):
    nd = lax.axis_size(DP)
    ns = lax.axis_size(SEQ)
    ny = lax.axis_size("y")
    nz = lax.axis_size("z")
    _, rows, width = inputs.shape
    blocks, part, length = first_factor.shape
    cols, part2, size2 = second_factor.shape
    crows, cpart = gate_weight.shape
    x = inputs.reshape(blocks, length, width)
    cot = out_grad.reshape(blocks, length, width)
    piece = shape((ns, blocks * cols, width), BF16)
    wide = 2 * rows * width * width
    cells = pltpu.VMEM((width // LANES, rows, LANES), F32)
    tail = cols * part2 * size2 // width
    both_rows = blocks * part + tail
    by_second = pl.BlockSpec((nd, tail, width), lambda i: (0, blocks * part // tail, 0))

    whole = shape((ns, 2 * blocks * cols, width), BF16)
    half = [
        pl.BlockSpec(piece.shape, functools.partial(lambda k, i: (0, k, 0), k)) for k in range(2)
    ]

    gate_part = exchange(jnp.broadcast_to(gate_weight[None], (nz, crows, cpart)), "z")
    weights = local(
        weights_kernel, shape((nd, both_rows, width), BF16), [first_factor, second_factor]
    )
    weights, gate_part = lax.optimization_barrier((weights, gate_part))
    weights = exchange(weights, DP)
    one = local(functools.partial(rows_kernel, cols), piece, [weights, x], flops=wide)
    one, gate_part = lax.optimization_barrier((one, gate_part))
    col_one = exchange(one, SEQ)

    gate_part = gather(gate_part, SEQ[1:]).transpose(1, 0, 2, 3).reshape(width, cpart)
    gate_full = gather(gate_part, DP).transpose(1, 0, 2).reshape(width, width)
    mixed_grad, slope = local(
        functools.partial(gate_kernel, cols),
        (whole, shape(x.shape, F32)),
        [x, gate_full, cot],
        out_specs=(half[0], VMEM),
        flops=wide,
    )
    both, by_col = local(
        forward_kernel,
        (whole, shape((cols, size2, width), BF16)),
        [weights, col_one, mixed_grad],
        [by_second, VMEM, ANY],
        (half[1], VMEM),
        flops=wide // 4,
        scratch=[cells, cells],
        alias={2: 0},
    )
    both = exchange(both, SEQ)
    col_back, spart = local(
        backward_kernel,
        (piece, shape((nd, tail, width), BF16)),
        [weights, both, by_col],
        [by_second, half[0], VMEM],
        flops=wide // 2,
        scratch=[cells, cells],
    )
    both, col_back = lax.optimization_barrier((both, col_back))
    back = exchange(col_back, SEQ)

    gate_input, keep, give = local(
        functools.partial(delta_kernel, cols),
        (
            shape(x.shape, BF16),
            shape((ny, cpart, width), F32),
            shape((ny, cpart, width), BF16),
        ),
        [lax.axis_index("xl")[None], both, slope, x, gate_full],
        [SMEM, half[1]] + [VMEM] * 3,
        flops=2 * wide,
        scratch=[pltpu.VMEM(x.shape, BF16), pltpu.VMEM((2, ny, cpart, width), F32)],
    )
    gsum = keep + swap(give, "xl", 1).astype(F32)
    keep, got = halve(gsum.reshape(2, ny // 2, cpart, width), "y", 2)
    keep, got = halve(keep + got, "y", 1)
    gsum = local(
        turn_kernel,
        shape((2, 2, nz, crows, cpart), F32),
        [keep, got],
    )
    keep, got = halve(gsum, "co", 1)
    keep, got = halve(keep + got, "xh", 1)
    bit = nz
    while bit > 4:
        bit //= 2
        keep, got = halve((keep + got).reshape(2, bit, crows, cpart), "z", bit)

    parts, by_row = local(
        functools.partial(outer_kernel, cols),
        (shape(weights.shape, BF16), shape(x.shape, BF16)),
        [back, x, spart],
        flops=wide,
    )
    keep, parts = lax.optimization_barrier((keep, parts))
    parts = exchange(parts, DP)
    while bit > 1:
        bit //= 2
        keep, got = halve((keep + got).reshape(2, bit, crows, cpart), "z", bit)
    grad_gate = (keep + got).reshape(crows, cpart)
    grad_inputs = local(inputs_kernel, shape(x.shape, BF16), [weights, by_row, gate_input], flops=wide)
    grad_first, grad_second = local(
        total_kernel, (shape(first_factor.shape, F32), shape(second_factor.shape, F32)), [parts]
    )
    return (grad_inputs.reshape(inputs.shape), grad_first, grad_second, grad_gate)


def solution(mesh):
    fine = Mesh(mesh.devices.reshape(16, 2, 2, 4, 2), SEQ + DP)
    specs = (P(SEQ, DP, None), P(SEQ, DP, None), P(SEQ, DP))
    return jax.shard_map(
        per_device,
        mesh=fine,
        in_specs=(P(DP, SEQ, None), P(DP, SEQ, None)) + specs,
        out_specs=(P(DP, SEQ, None),) + specs,
        check_vma=False,
    )
```

```python
import functools

import jax
import jax.numpy as jnp
from jax import lax
from jax.experimental import pallas as pl
from jax.experimental.pallas import tpu as pltpu
from jax.sharding import Mesh, PartitionSpec as P

BF16 = jnp.bfloat16
F32 = jnp.float32
SEQ = ("z", "xh", "co")
DP = ("y", "xl")
VMEM = pl.BlockSpec(memory_space=pltpu.VMEM)
ANY = pl.BlockSpec(memory_space=pl.ANY)
SMEM = pl.BlockSpec(memory_space=pltpu.SMEM)


def exchange(x, axis):
    return lax.all_to_all(x, axis, split_axis=0, concat_axis=0, tiled=True)


def gather(x, axes):
    out = x[None]
    for axis in reversed(axes):
        out = lax.all_gather(out, axis, axis=0, tiled=True)
    return out


def swap(x, axis, bits):
    n = lax.axis_size(axis)
    return lax.ppermute(x, axis, [(i, i ^ bits) for i in range(n)])


def local(body, out_shape, operands, in_specs=None, out_specs=None, flops=0, scratch=(), alias=None):
    outs = jax.tree.leaves(out_shape)
    moved = sum(a.size * a.dtype.itemsize for a in list(operands) + outs)
    return pl.pallas_call(
        body,
        grid=(1,),
        out_shape=out_shape,
        in_specs=in_specs or [VMEM] * len(operands),
        out_specs=out_specs or jax.tree.map(lambda _: VMEM, out_shape),
        input_output_aliases=alias or {},
        scratch_shapes=list(scratch),
        cost_estimate=pl.CostEstimate(flops=flops, bytes_accessed=moved, transcendentals=0),
        compiler_params=pltpu.CompilerParams(vmem_limit_bytes=28 << 20),
    )(*operands)


def shape(dims, dtype):
    return jax.ShapeDtypeStruct(dims, dtype)


def halve(x, axis, bit):
    low = lax.axis_index(axis) & bit == 0
    keep = jnp.where(low, x[0], x[1])
    give = jnp.where(low, x[1], x[0])
    return keep, swap(give, axis, bit)


def dot(a, b, ca=1, cb=0):
    return lax.dot_general(a, b, (((ca,), (cb,)), ((), ())), preferred_element_type=F32)


STEP = 32
LANES = 128


def lanes_of(x, k):
    return x[:, k * LANES : (k + 1) * LANES]


def pack(tops, cols, out_ref, start):
    tall = len(tops) * cols
    for k in range(tops[0].shape[1] // LANES):
        rows = [lanes_of(t, k).reshape(-1, cols, LANES) for t in tops]
        rows = jnp.concatenate(rows, axis=1).astype(BF16)
        out_ref[start : start + rows.shape[0], k * tall : (k + 1) * tall] = rows


def unpack(piece, cols, blocks, b):
    tall = blocks * cols
    rows = [
        piece[:, k * tall + b * cols : k * tall + (b + 1) * cols].reshape(-1, LANES)
        for k in range(piece.shape[1] // tall)
    ]
    return jnp.concatenate(rows, axis=1)


def beside(j, part, width):
    per = width // LANES
    return pl.ds((j // per) * part, part), pl.ds((j % per) * LANES, LANES)


def weights_kernel(first_ref, second_ref, out_ref):
    blocks, part, width = first_ref.shape
    for d in range(out_ref.shape[0]):
        for b in range(blocks):
            out_ref[d, b * part : (b + 1) * part] = first_ref[b]
        for j in range(second_ref.shape[0]):
            rows, lanes = beside(j, second_ref.shape[1], width)
            out_ref[d, pl.ds(blocks * part + rows.start, rows.size), lanes] = second_ref[j]


def second_of(second_ref, j):
    nd, _, width = second_ref.shape
    rows, lanes = beside(j, LANES // nd, width)
    return second_ref[:, rows, lanes].reshape(LANES, LANES)


def rows_kernel(cols, weights_ref, x_ref, gate_ref, out_ref):
    nd, (blocks, length, width) = weights_ref.shape[0], x_ref.shape
    part = length // nd
    per = STEP * cols // part
    body = width // LANES * blocks * cols
    rider = jnp.concatenate([gate_ref[...].astype(F32)] * 2, axis=1).astype(BF16)
    for c in range(out_ref.shape[0] // STEP):
        tops = []
        for b in range(blocks):
            mine = weights_ref[c * per : (c + 1) * per, b * part : (b + 1) * part]
            tops.append(dot(mine.reshape(per * part, length), x_ref[b]))
        pack(tops, cols, out_ref, c * STEP)
        out_ref[c * STEP : (c + 1) * STEP, body:] = jnp.broadcast_to(rider[None], (STEP,) + rider.shape)


def gate_kernel(cols, x_ref, weight_ref, cot_ref, out_ref, slope_ref):
    blocks = x_ref.shape[0]
    for c in range(out_ref.shape[0] // STEP):
        rows = pl.ds(c * STEP * cols, STEP * cols)
        tops = []
        for b in range(blocks):
            gate = jax.nn.sigmoid(dot(x_ref[b, rows], weight_ref[...]))
            grad = cot_ref[b, rows].astype(F32) * gate
            slope_ref[b, rows] = grad * (1.0 - gate)
            tops.append(grad)
        pack(tops, cols, out_ref, c * STEP)


def unfold(src_ref, tmp_ref):
    tall = tmp_ref.shape[1] // src_ref.shape[0]
    for c in range(0, src_ref.shape[0], STEP):
        for k in range(tmp_ref.shape[0]):
            piece = src_ref[c : c + STEP, k * tall : (k + 1) * tall].astype(F32)
            tmp_ref[k, pl.ds(c * tall, STEP * tall)] = piece.reshape(STEP * tall, LANES)


def fold(tmp_ref, dst_ref):
    tall = tmp_ref.shape[1] // dst_ref.shape[0]
    for c in range(0, dst_ref.shape[0], STEP):
        for k in range(tmp_ref.shape[0]):
            piece = tmp_ref[k, pl.ds(c * tall, STEP * tall)].reshape(STEP, tall, LANES)
            dst_ref[c : c + STEP, k * tall : (k + 1) * tall] = piece.astype(BF16)


def column(tmp_ref, j, cols):
    rows = pl.ds(j, tmp_ref.shape[1] // cols, stride=cols)
    return jnp.concatenate([tmp_ref[k, rows] for k in range(tmp_ref.shape[0])], axis=1)


def set_column(tmp_ref, j, cols, value):
    rows = pl.ds(j, tmp_ref.shape[1] // cols, stride=cols)
    for k in range(tmp_ref.shape[0]):
        tmp_ref[k, rows] = lanes_of(value, k)


def forward_kernel(second_ref, one_ref, two_ref, by_ref, tmp_ref, res_ref):
    unfold(one_ref, tmp_ref)
    cols = by_ref.shape[0]
    for j in range(cols):
        mine = column(tmp_ref, j, cols).astype(BF16)
        by_ref[j] = mine
        set_column(res_ref, j, cols, dot(second_of(second_ref, j), mine))
    fold(res_ref, two_ref)


def backward_kernel(second_ref, grad_ref, by_ref, keep_ref, got_ref, back_ref, part_ref, tmp_ref, res_ref):
    unfold(grad_ref, tmp_ref)
    cols = by_ref.shape[0]
    nd, _, width = part_ref.shape
    for j in range(cols):
        mine = column(tmp_ref, j, cols).astype(BF16)
        set_column(res_ref, j, cols, dot(second_of(second_ref, j), mine, 0, 0))
        rows, lanes = beside(j, LANES // nd, width)
        part = dot(mine, by_ref[j], 1, 1).reshape(nd, LANES // nd, LANES)
        part_ref[:, rows, lanes] = part.astype(BF16)
    fold(res_ref, back_ref)
    body = grad_ref.shape[1]
    total = (keep_ref[...] + got_ref[...]).T
    coarse = total.astype(BF16).astype(F32)
    rider = jnp.concatenate([coarse, total - coarse], axis=1)
    rider = rider.reshape(back_ref.shape[0], back_ref.shape[1] - body, LANES)
    back_ref[:, body:] = rider.astype(BF16)


def delta_kernel(
    cols, me_ref, two_ref, slope_ref, x_ref, weight_ref, input_ref, keep_ref, give_ref, delta_ref, sum_ref
):
    blocks, length, _ = x_ref.shape
    n = STEP * cols
    for c in range(two_ref.shape[0] // STEP):
        two = two_ref[c * STEP : (c + 1) * STEP].astype(F32)
        for b in range(blocks):
            rows = pl.ds(c * n, n)
            mine = unpack(two, cols, blocks, b)
            delta_ref[b, rows] = (mine * slope_ref[b, rows]).astype(BF16)
    pairs, cpart, width = keep_ref.shape
    for b in range(blocks):
        add = dot(delta_ref[b], x_ref[b], 0, 0).reshape(pairs, 2, cpart, width)
        for k in range(2):
            sum_ref[k] = add[:, k] if b == 0 else sum_ref[k] + add[:, k]
        input_ref[b] = dot(delta_ref[b], weight_ref[...], 1, 1).astype(BF16)
    keep_ref[...] = sum_ref[me_ref[0]]
    give_ref[...] = sum_ref[1 - me_ref[0]].astype(BF16)


def outer_kernel(cols, back_ref, x_ref, second_ref, part_ref, by_ref):
    blocks, length, _ = x_ref.shape
    nd, rows, width = part_ref.shape
    part = length // nd
    piece = back_ref[...].astype(F32)
    for b in range(blocks):
        by_ref[b] = unpack(piece, cols, blocks, b).astype(BF16)
        add = dot(by_ref[b], x_ref[b], 1, 1).astype(BF16)
        part_ref[:, b * part : (b + 1) * part] = add.reshape(nd, part, width)
    part_ref[:, blocks * part :] = second_ref[...]


def gate_sum_kernel(riders_ref, out_ref):
    total = jnp.sum(riders_ref[...].astype(F32), axis=0)
    half = out_ref.shape[1]
    out_ref[...] = total[:, :half] + total[:, half:]


def inputs_kernel(weights_ref, by_ref, input_ref, out_ref):
    nd, (blocks, length, _) = weights_ref.shape[0], by_ref.shape
    part = length // nd
    for b in range(blocks):
        mine = weights_ref[:, b * part : (b + 1) * part].reshape(length, length)
        through = dot(mine, by_ref[b], 0, 0)
        out_ref[b] = (through + input_ref[b].astype(F32)).astype(BF16)


def total_kernel(parts_ref, first_ref, second_ref):
    nd, _, width = parts_ref.shape
    blocks, part, _ = first_ref.shape
    for b in range(blocks):
        rows = pl.ds(b * part, part)
        first_ref[b] = sum(parts_ref[d, rows].astype(F32) for d in range(nd))
    for j in range(second_ref.shape[0]):
        rows, lanes = beside(j, second_ref.shape[1], width)
        rows = pl.ds(blocks * part + rows.start, rows.size)
        second_ref[j] = sum(parts_ref[d, rows, lanes].astype(F32) for d in range(nd))


def per_device(inputs, out_grad, first_factor, second_factor, gate_weight):
    nd = lax.axis_size(DP)
    ns = lax.axis_size(SEQ)
    ny = lax.axis_size("y")
    _, rows, width = inputs.shape
    blocks, part, length = first_factor.shape
    cols, part2, size2 = second_factor.shape
    crows, cpart = gate_weight.shape
    x = inputs.reshape(blocks, length, width)
    cot = out_grad.reshape(blocks, length, width)
    body = width // LANES * blocks * cols
    piece = shape((ns, body, LANES), BF16)
    longer = shape((ns, body + crows, LANES), BF16)
    wide = 2 * rows * width * width
    cells = pltpu.VMEM((width // LANES, rows, LANES), F32)
    tail = cols * part2 * size2 // width
    both_rows = blocks * part + tail
    by_second = pl.BlockSpec((nd, tail, width), lambda i: (0, blocks * part // tail, 0))
    by_body = pl.BlockSpec(piece.shape, lambda i: (0, 0, 0))
    by_rider = pl.BlockSpec((ns, crows, LANES), lambda i: (0, body // crows, 0))

    weights = local(
        weights_kernel, shape((nd, both_rows, width), BF16), [first_factor, second_factor]
    )
    weights = exchange(weights, DP)
    one = local(
        functools.partial(rows_kernel, cols), longer, [weights, x, gate_weight], flops=wide
    )
    col_one = exchange(one, SEQ)
    col_two, by_col = local(
        forward_kernel,
        (piece, shape((cols, size2, width), BF16)),
        [weights, col_one],
        [by_second, by_body],
        flops=wide // 4,
        scratch=[cells, cells],
    )
    col_one, col_two = lax.optimization_barrier((col_one, col_two))
    two = exchange(col_two, SEQ)

    gate_part = col_one[:, body:, :cpart].reshape(width, cpart)
    gate_full = gather(gate_part, DP).transpose(1, 0, 2).reshape(width, width)
    mixed_grad, slope = local(
        functools.partial(gate_kernel, cols),
        (piece, shape(x.shape, F32)),
        [x, gate_full, cot],
        flops=wide,
    )
    two, mixed_grad = lax.optimization_barrier((two, mixed_grad))
    col_grad = exchange(mixed_grad, SEQ)

    gate_input, keep, give = local(
        functools.partial(delta_kernel, cols),
        (
            shape(x.shape, BF16),
            shape((ny, cpart, width), F32),
            shape((ny, cpart, width), BF16),
        ),
        [lax.axis_index("xl")[None], two, slope, x, gate_full],
        [SMEM] + [VMEM] * 4,
        flops=2 * wide,
        scratch=[pltpu.VMEM(x.shape, BF16), pltpu.VMEM((2, ny, cpart, width), F32)],
    )
    gsum = keep + swap(give, "xl", 1).astype(F32)
    keep, got = halve(gsum.reshape(2, ny // 2, cpart, width), "y", 2)
    keep, got = halve(keep + got, "y", 1)
    col_grad, keep, got = lax.optimization_barrier((col_grad, keep, got))

    col_back, spart = local(
        backward_kernel,
        (longer, shape((nd, tail, width), BF16)),
        [weights, col_grad, by_col, keep, got],
        [by_second] + [VMEM] * 4,
        flops=wide // 2,
        scratch=[cells, cells],
    )
    back = exchange(col_back, SEQ)

    parts, by_row = local(
        functools.partial(outer_kernel, cols),
        (shape(weights.shape, BF16), shape(x.shape, BF16)),
        [back, x, spart],
        [by_body, VMEM, VMEM],
        flops=wide,
    )
    back, parts = lax.optimization_barrier((back, parts))
    parts = exchange(parts, DP)
    grad_gate = local(gate_sum_kernel, shape(gate_weight.shape, F32), [back], [by_rider])
    grad_inputs = local(inputs_kernel, shape(x.shape, BF16), [weights, by_row, gate_input], flops=wide)
    grad_first, grad_second = local(
        total_kernel, (shape(first_factor.shape, F32), shape(second_factor.shape, F32)), [parts]
    )
    return (grad_inputs.reshape(inputs.shape), grad_first, grad_second, grad_gate)


def solution(mesh):
    fine = Mesh(mesh.devices.reshape(16, 2, 2, 4, 2), SEQ + DP)
    specs = (P(SEQ, DP, None), P(SEQ, DP, None), P(SEQ, DP))
    return jax.shard_map(
        per_device,
        mesh=fine,
        in_specs=(P(DP, SEQ, None), P(DP, SEQ, None)) + specs,
        out_specs=(P(DP, SEQ, None),) + specs,
        check_vma=False,
    )
```

```python
import functools

import jax
import jax.numpy as jnp
from jax import lax
from jax.experimental import pallas as pl
from jax.experimental.pallas import tpu as pltpu
from jax.sharding import Mesh, PartitionSpec as P

BF16 = jnp.bfloat16
F32 = jnp.float32
SEQ = ("z", "xh", "co")
SENT = SEQ[::-1]
DP = ("y", "xl")
VMEM = pl.BlockSpec(memory_space=pltpu.VMEM)
ANY = pl.BlockSpec(memory_space=pl.ANY)
SMEM = pl.BlockSpec(memory_space=pltpu.SMEM)


def exchange(x, axis):
    return lax.all_to_all(x, axis, split_axis=0, concat_axis=0, tiled=True)


def gather(x, axes):
    out = x[None]
    for axis in reversed(axes):
        out = lax.all_gather(out, axis, axis=0, tiled=True)
    return out


def swap(x, axis, bits):
    n = lax.axis_size(axis)
    return lax.ppermute(x, axis, [(i, i ^ bits) for i in range(n)])


def local(body, out_shape, operands, in_specs=None, out_specs=None, flops=0, scratch=(), alias=None):
    outs = jax.tree.leaves(out_shape)
    moved = sum(a.size * a.dtype.itemsize for a in list(operands) + outs)
    return pl.pallas_call(
        body,
        grid=(1,),
        out_shape=out_shape,
        in_specs=in_specs or [VMEM] * len(operands),
        out_specs=out_specs or jax.tree.map(lambda _: VMEM, out_shape),
        input_output_aliases=alias or {},
        scratch_shapes=list(scratch),
        cost_estimate=pl.CostEstimate(flops=flops, bytes_accessed=moved, transcendentals=0),
        compiler_params=pltpu.CompilerParams(vmem_limit_bytes=28 << 20),
    )(*operands)


def shape(dims, dtype):
    return jax.ShapeDtypeStruct(dims, dtype)


def halve(x, axis, bit):
    low = lax.axis_index(axis) & bit == 0
    keep = jnp.where(low, x[0], x[1])
    give = jnp.where(low, x[1], x[0])
    return keep, swap(give, axis, bit)


def dot(a, b, ca=1, cb=0):
    return lax.dot_general(a, b, (((ca,), (cb,)), ((), ())), preferred_element_type=F32)


STEP = 32
LANES = 128


def lanes_of(x, k):
    return x[:, k * LANES : (k + 1) * LANES]


def lanes_of(x, k):
    return x[:, k * LANES : (k + 1) * LANES]


def slot(owner):
    return lambda n: (owner % 2) * (n // 2) + (owner // 2 % 2) * (n // 4) + owner // 4


def pack(tops, cols, out_ref, start):
    tall = len(tops) * cols
    for k in range(tops[0].shape[1] // LANES):
        rows = [lanes_of(t, k).reshape(-1, cols, LANES) for t in tops]
        rows = jnp.concatenate(rows, axis=1).astype(BF16)
        for i in range(rows.shape[0]):
            out_ref[slot(start + i)(out_ref.shape[0]), k * tall : (k + 1) * tall] = rows[i]


def unpack(src_ref, start, count, cols, blocks, b):
    tall = blocks * cols
    piece = jnp.stack([src_ref[slot(s)(src_ref.shape[0])] for s in range(start, start + count)])
    piece = piece.astype(F32)
    rows = [
        piece[:, k * tall + b * cols : k * tall + (b + 1) * cols].reshape(-1, LANES)
        for k in range(piece.shape[1] // tall)
    ]
    return jnp.concatenate(rows, axis=1)


def beside(j, part, width):
    per = width // LANES
    return pl.ds((j // per) * part, part), pl.ds((j % per) * LANES, LANES)


def weights_kernel(first_ref, second_ref, out_ref):
    blocks, part, width = first_ref.shape
    for d in range(out_ref.shape[0]):
        for b in range(blocks):
            out_ref[d, b * part : (b + 1) * part] = first_ref[b]
        for j in range(second_ref.shape[0]):
            rows, lanes = beside(j, second_ref.shape[1], width)
            out_ref[d, pl.ds(blocks * part + rows.start, rows.size), lanes] = second_ref[j]


def second_of(second_ref, j):
    nd, _, width = second_ref.shape
    rows, lanes = beside(j, LANES // nd, width)
    return second_ref[:, rows, lanes].reshape(LANES, LANES)


def rows_kernel(cols, weights_ref, x_ref, gate_ref, out_ref):
    nd, (blocks, length, width) = weights_ref.shape[0], x_ref.shape
    part = length // nd
    per = STEP * cols // part
    body = width // LANES * blocks * cols
    rider = jnp.concatenate([gate_ref[...].astype(F32)] * 2, axis=1).astype(BF16)
    for c in range(out_ref.shape[0] // STEP):
        tops = []
        for b in range(blocks):
            mine = weights_ref[c * per : (c + 1) * per, b * part : (b + 1) * part]
            tops.append(dot(mine.reshape(per * part, length), x_ref[b]))
        pack(tops, cols, out_ref, c * STEP)
        out_ref[c * STEP : (c + 1) * STEP, body:] = jnp.broadcast_to(rider[None], (STEP,) + rider.shape)


def gate_kernel(cols, x_ref, weight_ref, cot_ref, out_ref, slope_ref):
    blocks = x_ref.shape[0]
    for c in range(out_ref.shape[0] // STEP):
        rows = pl.ds(c * STEP * cols, STEP * cols)
        tops = []
        for b in range(blocks):
            gate = jax.nn.sigmoid(dot(x_ref[b, rows], weight_ref[...]))
            grad = cot_ref[b, rows].astype(F32) * gate
            slope_ref[b, rows] = grad * (1.0 - gate)
            tops.append(grad)
        pack(tops, cols, out_ref, c * STEP)


def unfold(src_ref, tmp_ref):
    n = src_ref.shape[0]
    tall = tmp_ref.shape[1] // n
    for s in range(n):
        for k in range(tmp_ref.shape[0]):
            piece = src_ref[slot(s)(n), k * tall : (k + 1) * tall]
            tmp_ref[k, pl.ds(s * tall, tall)] = piece.astype(F32)


def fold(tmp_ref, dst_ref):
    n = dst_ref.shape[0]
    tall = tmp_ref.shape[1] // n
    for s in range(n):
        for k in range(tmp_ref.shape[0]):
            piece = tmp_ref[k, pl.ds(s * tall, tall)].astype(BF16)
            dst_ref[slot(s)(n), k * tall : (k + 1) * tall] = piece


def column(tmp_ref, j, cols):
    rows = pl.ds(j, tmp_ref.shape[1] // cols, stride=cols)
    return jnp.concatenate([tmp_ref[k, rows] for k in range(tmp_ref.shape[0])], axis=1)


def set_column(tmp_ref, j, cols, value):
    rows = pl.ds(j, tmp_ref.shape[1] // cols, stride=cols)
    for k in range(tmp_ref.shape[0]):
        tmp_ref[k, rows] = lanes_of(value, k)


def columns_kernel(one_ref, by_ref, tmp_ref):
    unfold(one_ref, tmp_ref)
    for j in range(by_ref.shape[0]):
        by_ref[j] = column(tmp_ref, j, by_ref.shape[0]).astype(BF16)


def forward_kernel(cols, second_ref, one_ref, two_ref, tmp_ref, res_ref):
    unfold(one_ref, tmp_ref)
    for j in range(cols):
        mine = column(tmp_ref, j, cols).astype(BF16)
        set_column(res_ref, j, cols, dot(second_of(second_ref, j), mine))
    fold(res_ref, two_ref)


def backward_kernel(second_ref, grad_ref, by_ref, keep_ref, got_ref, back_ref, part_ref, tmp_ref, res_ref):
    unfold(grad_ref, tmp_ref)
    cols = by_ref.shape[0]
    nd, _, width = part_ref.shape
    for j in range(cols):
        mine = column(tmp_ref, j, cols).astype(BF16)
        set_column(res_ref, j, cols, dot(second_of(second_ref, j), mine, 0, 0))
        rows, lanes = beside(j, LANES // nd, width)
        part = dot(mine, by_ref[j], 1, 1).reshape(nd, LANES // nd, LANES)
        part_ref[:, rows, lanes] = part.astype(BF16)
    fold(res_ref, back_ref)
    body = grad_ref.shape[1]
    total = (keep_ref[...] + got_ref[...]).T
    coarse = total.astype(BF16).astype(F32)
    rider = jnp.concatenate([coarse, total - coarse], axis=1)
    n = back_ref.shape[0]
    rider = rider.reshape(n, back_ref.shape[1] - body, LANES).astype(BF16)
    for s in range(n):
        back_ref[slot(s)(n), body:] = rider[s]


def delta_kernel(
    cols, me_ref, two_ref, slope_ref, x_ref, weight_ref, input_ref, keep_ref, give_ref, delta_ref, sum_ref
):
    blocks, length, _ = x_ref.shape
    n = STEP * cols
    for c in range(two_ref.shape[0] // STEP):
        for b in range(blocks):
            rows = pl.ds(c * n, n)
            mine = unpack(two_ref, c * STEP, STEP, cols, blocks, b)
            delta_ref[b, rows] = (mine * slope_ref[b, rows]).astype(BF16)
    pairs, cpart, width = keep_ref.shape
    for b in range(blocks):
        add = dot(delta_ref[b], x_ref[b], 0, 0).reshape(pairs, 2, cpart, width)
        for k in range(2):
            sum_ref[k] = add[:, k] if b == 0 else sum_ref[k] + add[:, k]
        input_ref[b] = dot(delta_ref[b], weight_ref[...], 1, 1).astype(BF16)
    keep_ref[...] = sum_ref[me_ref[0]]
    give_ref[...] = sum_ref[1 - me_ref[0]].astype(BF16)


def outer_kernel(cols, back_ref, x_ref, second_ref, part_ref):
    blocks, length, _ = x_ref.shape
    nd, rows, width = part_ref.shape
    part = length // nd
    for b in range(blocks):
        mine = unpack(back_ref, 0, back_ref.shape[0], cols, blocks, b).astype(BF16)
        add = dot(mine, x_ref[b], 1, 1).astype(BF16)
        part_ref[:, b * part : (b + 1) * part] = add.reshape(nd, part, width)
    part_ref[:, blocks * part :] = second_ref[...]


def gate_sum_kernel(riders_ref, out_ref):
    total = jnp.sum(riders_ref[...].astype(F32), axis=0)
    half = out_ref.shape[1]
    out_ref[...] = total[:, :half] + total[:, half:]


def inputs_kernel(cols, weights_ref, back_ref, input_ref, out_ref):
    nd, (blocks, length, _) = weights_ref.shape[0], out_ref.shape
    part = length // nd
    for b in range(blocks):
        mine = weights_ref[:, b * part : (b + 1) * part].reshape(length, length)
        back = unpack(back_ref, 0, back_ref.shape[0], cols, blocks, b).astype(BF16)
        through = dot(mine, back, 0, 0)
        out_ref[b] = (through + input_ref[b].astype(F32)).astype(BF16)


def total_kernel(parts_ref, first_ref, second_ref):
    nd, _, width = parts_ref.shape
    blocks, part, _ = first_ref.shape
    for b in range(blocks):
        rows = pl.ds(b * part, part)
        first_ref[b] = sum(parts_ref[d, rows].astype(F32) for d in range(nd))
    for j in range(second_ref.shape[0]):
        rows, lanes = beside(j, second_ref.shape[1], width)
        rows = pl.ds(blocks * part + rows.start, rows.size)
        second_ref[j] = sum(parts_ref[d, rows, lanes].astype(F32) for d in range(nd))


def per_device(inputs, out_grad, first_factor, second_factor, gate_weight):
    nd = lax.axis_size(DP)
    ns = lax.axis_size(SEQ)
    ny = lax.axis_size("y")
    _, rows, width = inputs.shape
    blocks, part, length = first_factor.shape
    cols, part2, size2 = second_factor.shape
    crows, cpart = gate_weight.shape
    x = inputs.reshape(blocks, length, width)
    cot = out_grad.reshape(blocks, length, width)
    body = width // LANES * blocks * cols
    piece = shape((ns, body, LANES), BF16)
    longer = shape((ns, body + crows, LANES), BF16)
    wide = 2 * rows * width * width
    cells = pltpu.VMEM((width // LANES, rows, LANES), F32)
    tail = cols * part2 * size2 // width
    both_rows = blocks * part + tail
    by_second = pl.BlockSpec((nd, tail, width), lambda i: (0, blocks * part // tail, 0))
    by_body = pl.BlockSpec(piece.shape, lambda i: (0, 0, 0))
    by_rider = pl.BlockSpec((ns, crows, LANES), lambda i: (0, body // crows, 0))

    weights = local(
        weights_kernel, shape((nd, both_rows, width), BF16), [first_factor, second_factor]
    )
    weights = exchange(weights, DP)
    one = local(
        functools.partial(rows_kernel, cols), longer, [weights, x, gate_weight], flops=wide
    )
    col_one = exchange(one, SENT)
    col_two = local(
        functools.partial(forward_kernel, cols),
        piece,
        [weights, col_one],
        [by_second, by_body],
        flops=wide // 4,
        scratch=[cells, cells],
    )
    col_one, col_two = lax.optimization_barrier((col_one, col_two))
    two = exchange(col_two, SENT)
    by_col = local(
        columns_kernel, shape((cols, size2, width), BF16), [col_one], [by_body], scratch=[cells]
    )

    gate_part = col_one[:, body:, :cpart].reshape(2, 2, ns // 4, crows, cpart)
    gate_part = gate_part.transpose(2, 1, 0, 3, 4).reshape(width, cpart)
    gate_full = gather(gate_part, DP).transpose(1, 0, 2).reshape(width, width)
    mixed_grad, slope = local(
        functools.partial(gate_kernel, cols),
        (piece, shape(x.shape, F32)),
        [x, gate_full, cot],
        flops=wide,
    )
    two, mixed_grad = lax.optimization_barrier((two, mixed_grad))
    col_grad = exchange(mixed_grad, SENT)

    gate_input, keep, give = local(
        functools.partial(delta_kernel, cols),
        (
            shape(x.shape, BF16),
            shape((ny, cpart, width), F32),
            shape((ny, cpart, width), BF16),
        ),
        [lax.axis_index("xl")[None], two, slope, x, gate_full],
        [SMEM] + [VMEM] * 4,
        flops=2 * wide,
        scratch=[pltpu.VMEM(x.shape, BF16), pltpu.VMEM((2, ny, cpart, width), F32)],
    )
    gsum = keep + swap(give, "xl", 1).astype(F32)
    keep, got = halve(gsum.reshape(2, ny // 2, cpart, width), "y", 2)
    keep, got = halve(keep + got, "y", 1)
    col_grad, keep, got = lax.optimization_barrier((col_grad, keep, got))

    col_back, spart = local(
        backward_kernel,
        (longer, shape((nd, tail, width), BF16)),
        [weights, col_grad, by_col, keep, got],
        [by_second] + [VMEM] * 4,
        flops=wide // 2,
        scratch=[cells, cells],
    )
    back = exchange(col_back, SENT)

    parts = local(
        functools.partial(outer_kernel, cols),
        shape(weights.shape, BF16),
        [back, x, spart],
        [by_body, VMEM, VMEM],
        flops=wide,
    )
    back, parts = lax.optimization_barrier((back, parts))
    parts = exchange(parts, DP)
    grad_gate = local(gate_sum_kernel, shape(gate_weight.shape, F32), [back], [by_rider])
    grad_inputs = local(
        functools.partial(inputs_kernel, cols),
        shape(x.shape, BF16),
        [weights, back, gate_input],
        [VMEM, by_body, VMEM],
        flops=wide,
    )
    grad_first, grad_second = local(
        total_kernel, (shape(first_factor.shape, F32), shape(second_factor.shape, F32)), [parts]
    )
    return (grad_inputs.reshape(inputs.shape), grad_first, grad_second, grad_gate)


def solution(mesh):
    fine = Mesh(mesh.devices.reshape(16, 2, 2, 4, 2), SEQ + DP)
    specs = (P(SEQ, DP, None), P(SEQ, DP, None), P(SEQ, DP))
    return jax.shard_map(
        per_device,
        mesh=fine,
        in_specs=(P(DP, SEQ, None), P(DP, SEQ, None)) + specs,
        out_specs=(P(DP, SEQ, None),) + specs,
        check_vma=False,
    )
```

```python
import functools

import jax
import jax.numpy as jnp
from jax import lax
from jax.experimental import pallas as pl
from jax.experimental.pallas import tpu as pltpu
from jax.sharding import Mesh, PartitionSpec as P

BF16 = jnp.bfloat16
F32 = jnp.float32
SEQ = ("z", "xh", "co")
DP = ("y", "xl")
VMEM = pl.BlockSpec(memory_space=pltpu.VMEM)
HBM = pl.BlockSpec(memory_space=pltpu.HBM)
SMEM = pl.BlockSpec(memory_space=pltpu.SMEM)


def exchange(x, axis):
    return lax.all_to_all(x, axis, split_axis=0, concat_axis=0, tiled=True)


def gather(x, axes):
    out = x[None]
    for axis in reversed(axes):
        out = lax.all_gather(out, axis, axis=0, tiled=True)
    return out


def swap(x, axis, bits):
    n = lax.axis_size(axis)
    return lax.ppermute(x, axis, [(i, i ^ bits) for i in range(n)])


def local(body, out_shape, operands, in_specs=None, out_specs=None, flops=0, scratch=(), room=60):
    outs = jax.tree.leaves(out_shape)
    moved = sum(a.size * a.dtype.itemsize for a in list(operands) + outs)
    return pl.pallas_call(
        body,
        grid=(1,),
        out_shape=out_shape,
        in_specs=in_specs or [VMEM] * len(operands),
        out_specs=out_specs or jax.tree.map(lambda _: VMEM, out_shape),
        scratch_shapes=list(scratch),
        cost_estimate=pl.CostEstimate(flops=flops, bytes_accessed=moved, transcendentals=0),
        compiler_params=pltpu.CompilerParams(vmem_limit_bytes=room << 20),
    )(*operands)


def shape(dims, dtype):
    return jax.ShapeDtypeStruct(dims, dtype)


def halve(x, axis, bit):
    low = lax.axis_index(axis) & bit == 0
    keep = jnp.where(low, x[0], x[1])
    give = jnp.where(low, x[1], x[0])
    return keep, swap(give, axis, bit)


def dot(a, b, ca=1, cb=0):
    return lax.dot_general(a, b, (((ca,), (cb,)), ((), ())), preferred_element_type=F32)


STEP = 32
LANES = 128


def lanes_of(x, k):
    return x[:, k * LANES : (k + 1) * LANES]


def lanes_of(x, k):
    return x[:, k * LANES : (k + 1) * LANES]


def pack(tops, cols, out_ref, start):
    tall = len(tops) * cols
    for k in range(tops[0].shape[1] // LANES):
        rows = [lanes_of(t, k).reshape(-1, cols, LANES) for t in tops]
        rows = jnp.concatenate(rows, axis=1).astype(BF16)
        out_ref[start : start + rows.shape[0], k * tall : (k + 1) * tall] = rows


def unpack(src_ref, start, count, cols, blocks, b):
    tall = blocks * cols
    piece = src_ref[start : start + count].astype(F32)
    rows = [
        piece[:, k * tall + b * cols : k * tall + (b + 1) * cols].reshape(-1, LANES)
        for k in range(piece.shape[1] // tall)
    ]
    return jnp.concatenate(rows, axis=1)


def beside(j, part, width):
    per = width // LANES
    return pl.ds((j // per) * part, part), pl.ds((j % per) * LANES, LANES)


def weights_kernel(first_ref, second_ref, out_ref):
    blocks, part, width = first_ref.shape
    for d in range(out_ref.shape[0]):
        for b in range(blocks):
            out_ref[d, b * part : (b + 1) * part] = first_ref[b]
        for j in range(second_ref.shape[0]):
            rows, lanes = beside(j, second_ref.shape[1], width)
            out_ref[d, pl.ds(blocks * part + rows.start, rows.size), lanes] = second_ref[j]


def second_of(second_ref, j):
    nd, _, width = second_ref.shape
    rows, lanes = beside(j, LANES // nd, width)
    return second_ref[:, rows, lanes].reshape(LANES, LANES)


def rows_kernel(cols, weights_ref, x_ref, gate_ref, out_ref):
    nd, (blocks, length, width) = weights_ref.shape[0], x_ref.shape
    part = length // nd
    per = STEP * cols // part
    body = width // LANES * blocks * cols
    rider = jnp.concatenate([gate_ref[...].astype(F32)] * 2, axis=1).astype(BF16)
    for c in range(out_ref.shape[0] // STEP):
        tops = []
        for b in range(blocks):
            mine = weights_ref[c * per : (c + 1) * per, b * part : (b + 1) * part]
            tops.append(dot(mine.reshape(per * part, length), x_ref[b]))
        pack(tops, cols, out_ref, c * STEP)
        out_ref[c * STEP : (c + 1) * STEP, body:] = jnp.broadcast_to(rider[None], (STEP,) + rider.shape)


def gate_kernel(cols, x_ref, weight_ref, cot_ref, out_ref, slope_ref):
    blocks = x_ref.shape[0]
    for c in range(out_ref.shape[0] // STEP):
        rows = pl.ds(c * STEP * cols, STEP * cols)
        tops = []
        for b in range(blocks):
            gate = jax.nn.sigmoid(dot(x_ref[b, rows], weight_ref[...]))
            grad = cot_ref[b, rows].astype(F32) * gate
            slope_ref[b, rows] = grad * (1.0 - gate)
            tops.append(grad)
        pack(tops, cols, out_ref, c * STEP)


def unfold(src_ref, tmp_ref):
    tall = tmp_ref.shape[1] // src_ref.shape[0]
    for c in range(0, src_ref.shape[0], STEP):
        for k in range(tmp_ref.shape[0]):
            piece = src_ref[c : c + STEP, k * tall : (k + 1) * tall].astype(F32)
            tmp_ref[k, pl.ds(c * tall, STEP * tall)] = piece.reshape(STEP * tall, LANES)


def fold(tmp_ref, dst_ref, start):
    tall = tmp_ref.shape[1] // dst_ref.shape[0]
    for k in range(tmp_ref.shape[0]):
        piece = tmp_ref[k, pl.ds(start * tall, STEP * tall)].reshape(STEP, tall, LANES)
        dst_ref[start : start + STEP, k * tall : (k + 1) * tall] = piece.astype(BF16)


def column(tmp_ref, j, cols):
    rows = pl.ds(j, tmp_ref.shape[1] // cols, stride=cols)
    return jnp.concatenate([tmp_ref[k, rows] for k in range(tmp_ref.shape[0])], axis=1)


def set_column(tmp_ref, j, cols, value):
    rows = pl.ds(j, tmp_ref.shape[1] // cols, stride=cols)
    for k in range(tmp_ref.shape[0]):
        tmp_ref[k, rows] = lanes_of(value, k)


def columns_kernel(one_ref, by_ref, tmp_ref):
    unfold(one_ref, tmp_ref)
    for j in range(by_ref.shape[0]):
        by_ref[j] = column(tmp_ref, j, by_ref.shape[0]).astype(BF16)


def forward_kernel(cols, second_ref, one_ref, two_ref, tmp_ref, res_ref, done_ref, sems):
    unfold(one_ref, tmp_ref)
    for j in range(cols):
        mine = column(tmp_ref, j, cols).astype(BF16)
        set_column(res_ref, j, cols, dot(second_of(second_ref, j), mine))
    copies = []
    for i, c in enumerate(range(0, done_ref.shape[0], STEP)):
        fold(res_ref, done_ref, c)
        here = pl.ds(c, STEP)
        copies.append(pltpu.make_async_copy(done_ref.at[here], two_ref.at[here], sems.at[i]))
        copies[-1].start()
    for copy in copies:
        copy.wait()


def backward_kernel(
    second_ref, grad_ref, by_ref, keep_ref, got_ref, back_ref, part_ref,
    tmp_ref, res_ref, mine_ref, sums_ref, sems,
):
    copies = [
        pltpu.make_async_copy(by_ref, mine_ref, sems.at[0]),
        pltpu.make_async_copy(keep_ref, sums_ref.at[0], sems.at[1]),
        pltpu.make_async_copy(got_ref, sums_ref.at[1], sems.at[2]),
    ]
    for copy in copies:
        copy.start()
    unfold(grad_ref, tmp_ref)
    for copy in copies:
        copy.wait()
    cols = mine_ref.shape[0]
    nd, _, width = part_ref.shape
    for j in range(cols):
        mine = column(tmp_ref, j, cols).astype(BF16)
        set_column(res_ref, j, cols, dot(second_of(second_ref, j), mine, 0, 0))
        rows, lanes = beside(j, LANES // nd, width)
        part = dot(mine, mine_ref[j], 1, 1).reshape(nd, LANES // nd, LANES)
        part_ref[:, rows, lanes] = part.astype(BF16)
    body = grad_ref.shape[1]
    for c in range(0, grad_ref.shape[0], STEP):
        tall = tmp_ref.shape[1] // grad_ref.shape[0]
        for k in range(tmp_ref.shape[0]):
            piece = res_ref[k, pl.ds(c * tall, STEP * tall)].reshape(STEP, tall, LANES)
            back_ref[c : c + STEP, k * tall : (k + 1) * tall] = piece.astype(BF16)
    total = (sums_ref[0] + sums_ref[1]).T
    coarse = total.astype(BF16).astype(F32)
    rider = jnp.concatenate([coarse, total - coarse], axis=1)
    rider = rider.reshape(back_ref.shape[0], back_ref.shape[1] - body, LANES)
    back_ref[:, body:] = rider.astype(BF16)


def delta_kernel(
    cols, me_ref, two_ref, slope_ref, x_ref, weight_ref, input_ref, keep_ref, give_ref, delta_ref, sum_ref
):
    blocks, length, _ = x_ref.shape
    n = STEP * cols
    for c in range(two_ref.shape[0] // STEP):
        for b in range(blocks):
            rows = pl.ds(c * n, n)
            mine = unpack(two_ref, c * STEP, STEP, cols, blocks, b)
            delta_ref[b, rows] = (mine * slope_ref[b, rows]).astype(BF16)
    pairs, cpart, width = keep_ref.shape
    for b in range(blocks):
        add = dot(delta_ref[b], x_ref[b], 0, 0).reshape(pairs, 2, cpart, width)
        for k in range(2):
            sum_ref[k] = add[:, k] if b == 0 else sum_ref[k] + add[:, k]
        input_ref[b] = dot(delta_ref[b], weight_ref[...], 1, 1).astype(BF16)
    keep_ref[...] = sum_ref[me_ref[0]]
    give_ref[...] = sum_ref[1 - me_ref[0]].astype(BF16)


def outer_kernel(cols, back_ref, x_ref, second_ref, out_ref, part_ref, sems):
    blocks, length, _ = x_ref.shape
    nd, rows, width = part_ref.shape
    part = length // nd
    copies = [pltpu.make_async_copy(second_ref, out_ref.at[:, pl.ds(rows, second_ref.shape[1])], sems.at[0])]
    copies[0].start()
    for b in range(blocks):
        mine = unpack(back_ref, 0, back_ref.shape[0], cols, blocks, b).astype(BF16)
        add = dot(mine, x_ref[b], 1, 1).astype(BF16)
        here = pl.ds(b * part, part)
        part_ref[:, here] = add.reshape(nd, part, width)
        copies.append(pltpu.make_async_copy(part_ref.at[:, here], out_ref.at[:, here], sems.at[b + 1]))
        copies[-1].start()
    for copy in copies:
        copy.wait()


def gate_sum_kernel(riders_ref, out_ref):
    total = jnp.sum(riders_ref[...].astype(F32), axis=0)
    half = out_ref.shape[1]
    out_ref[...] = total[:, :half] + total[:, half:]


def inputs_kernel(cols, weights_ref, back_ref, input_ref, out_ref):
    nd, (blocks, length, _) = weights_ref.shape[0], out_ref.shape
    part = length // nd
    for b in range(blocks):
        mine = weights_ref[:, b * part : (b + 1) * part].reshape(length, length)
        back = unpack(back_ref, 0, back_ref.shape[0], cols, blocks, b).astype(BF16)
        through = dot(mine, back, 0, 0)
        out_ref[b] = (through + input_ref[b].astype(F32)).astype(BF16)


def total_kernel(parts_ref, first_ref, second_ref):
    nd, _, width = parts_ref.shape
    blocks, part, _ = first_ref.shape
    for b in range(blocks):
        rows = pl.ds(b * part, part)
        first_ref[b] = sum(parts_ref[d, rows].astype(F32) for d in range(nd))
    for j in range(second_ref.shape[0]):
        rows, lanes = beside(j, second_ref.shape[1], width)
        rows = pl.ds(blocks * part + rows.start, rows.size)
        second_ref[j] = sum(parts_ref[d, rows, lanes].astype(F32) for d in range(nd))


def per_device(inputs, out_grad, first_factor, second_factor, gate_weight):
    nd = lax.axis_size(DP)
    ns = lax.axis_size(SEQ)
    ny = lax.axis_size("y")
    _, rows, width = inputs.shape
    blocks, part, length = first_factor.shape
    cols, part2, size2 = second_factor.shape
    crows, cpart = gate_weight.shape
    x = inputs.reshape(blocks, length, width)
    cot = out_grad.reshape(blocks, length, width)
    body = width // LANES * blocks * cols
    piece = shape((ns, body, LANES), BF16)
    longer = shape((ns, body + crows, LANES), BF16)
    wide = 2 * rows * width * width
    cells = pltpu.VMEM((width // LANES, rows, LANES), F32)
    tail = cols * part2 * size2 // width
    both_rows = blocks * part + tail
    by_second = pl.BlockSpec((nd, tail, width), lambda i: (0, blocks * part // tail, 0))
    by_body = pl.BlockSpec(piece.shape, lambda i: (0, 0, 0))
    by_rider = pl.BlockSpec((ns, crows, LANES), lambda i: (0, body // crows, 0))

    weights = local(
        weights_kernel, shape((nd, both_rows, width), BF16), [first_factor, second_factor]
    )
    weights = exchange(weights, DP)
    one = local(
        functools.partial(rows_kernel, cols), longer, [weights, x, gate_weight], flops=wide
    )
    col_one = exchange(one, SEQ)
    col_two = local(
        functools.partial(forward_kernel, cols),
        piece,
        [weights, col_one],
        [by_second, by_body],
        HBM,
        flops=wide // 4,
        scratch=[cells, cells, pltpu.VMEM(piece.shape, BF16), pltpu.SemaphoreType.DMA((ns // STEP,))],
    )
    col_one, col_two = lax.optimization_barrier((col_one, col_two))
    two = exchange(col_two, SEQ)
    by_col = local(
        columns_kernel, shape((cols, size2, width), BF16), [col_one], [by_body], scratch=[cells]
    )

    gate_part = col_one[:, body:, :cpart].reshape(width, cpart)
    gate_full = gather(gate_part, DP).transpose(1, 0, 2).reshape(width, width)
    mixed_grad, slope = local(
        functools.partial(gate_kernel, cols),
        (piece, shape(x.shape, F32)),
        [x, gate_full, cot],
        flops=wide,
    )
    two, mixed_grad = lax.optimization_barrier((two, mixed_grad))
    col_grad = exchange(mixed_grad, SEQ)

    gate_input, keep, give = local(
        functools.partial(delta_kernel, cols),
        (
            shape(x.shape, BF16),
            shape((ny, cpart, width), F32),
            shape((ny, cpart, width), BF16),
        ),
        [lax.axis_index("xl")[None], two, slope, x, gate_full],
        [SMEM] + [VMEM] * 4,
        flops=2 * wide,
        scratch=[pltpu.VMEM(x.shape, BF16), pltpu.VMEM((2, ny, cpart, width), F32)],
        room=28,
    )
    gsum = keep + swap(give, "xl", 1).astype(F32)
    keep, got = halve(gsum.reshape(2, ny // 2, cpart, width), "y", 2)
    keep, got = halve(keep + got, "y", 1)
    col_grad, keep, got = lax.optimization_barrier((col_grad, keep, got))

    col_back, spart = local(
        backward_kernel,
        (longer, shape((nd, tail, width), BF16)),
        [weights, col_grad, by_col, keep, got],
        [by_second, VMEM, HBM, HBM, HBM],
        flops=wide // 2,
        scratch=[
            cells,
            cells,
            pltpu.VMEM((cols, size2, width), BF16),
            pltpu.VMEM((2, cpart, width), F32),
            pltpu.SemaphoreType.DMA((3,)),
        ],
    )
    back = exchange(col_back, SEQ)

    parts = local(
        functools.partial(outer_kernel, cols),
        shape(weights.shape, BF16),
        [back, x, spart],
        [by_body, VMEM, HBM],
        HBM,
        flops=wide,
        scratch=[
            pltpu.VMEM((nd, blocks * part, width), BF16),
            pltpu.SemaphoreType.DMA((blocks + 1,)),
        ],
    )
    back, parts = lax.optimization_barrier((back, parts))
    parts = exchange(parts, DP)
    grad_gate = local(gate_sum_kernel, shape(gate_weight.shape, F32), [back], [by_rider])
    grad_inputs = local(
        functools.partial(inputs_kernel, cols),
        shape(x.shape, BF16),
        [weights, back, gate_input],
        [VMEM, by_body, VMEM],
        flops=wide,
    )
    grad_first, grad_second = local(
        total_kernel, (shape(first_factor.shape, F32), shape(second_factor.shape, F32)), [parts], room=28
    )
    return (grad_inputs.reshape(inputs.shape), grad_first, grad_second, grad_gate)


def solution(mesh):
    fine = Mesh(mesh.devices.reshape(16, 2, 2, 4, 2), SEQ + DP)
    specs = (P(SEQ, DP, None), P(SEQ, DP, None), P(SEQ, DP))
    return jax.shard_map(
        per_device,
        mesh=fine,
        in_specs=(P(DP, SEQ, None), P(DP, SEQ, None)) + specs,
        out_specs=(P(DP, SEQ, None),) + specs,
        check_vma=False,
    )
```

```python
import functools

import jax
import jax.numpy as jnp
from jax import lax
from jax.experimental import pallas as pl
from jax.experimental.pallas import tpu as pltpu
from jax.sharding import Mesh, PartitionSpec as P

BF16 = jnp.bfloat16
F32 = jnp.float32
SEQ = ("z", "xh", "co")
DP = ("y", "xl")
VMEM = pl.BlockSpec(memory_space=pltpu.VMEM)
ANY = pl.BlockSpec(memory_space=pl.ANY)
SMEM = pl.BlockSpec(memory_space=pltpu.SMEM)


def exchange(x, axis):
    return lax.all_to_all(x, axis, split_axis=0, concat_axis=0, tiled=True)


def gather(x, axes):
    out = x[None]
    for axis in reversed(axes):
        out = lax.all_gather(out, axis, axis=0, tiled=True)
    return out


def swap(x, axis, bits):
    n = lax.axis_size(axis)
    return lax.ppermute(x, axis, [(i, i ^ bits) for i in range(n)])


def local(body, out_shape, operands, in_specs=None, out_specs=None, flops=0, scratch=(), alias=None):
    outs = jax.tree.leaves(out_shape)
    moved = sum(a.size * a.dtype.itemsize for a in list(operands) + outs)
    return pl.pallas_call(
        body,
        grid=(1,),
        out_shape=out_shape,
        in_specs=in_specs or [VMEM] * len(operands),
        out_specs=out_specs or jax.tree.map(lambda _: VMEM, out_shape),
        input_output_aliases=alias or {},
        scratch_shapes=list(scratch),
        cost_estimate=pl.CostEstimate(flops=flops, bytes_accessed=moved, transcendentals=0),
        compiler_params=pltpu.CompilerParams(vmem_limit_bytes=28 << 20),
    )(*operands)


def shape(dims, dtype):
    return jax.ShapeDtypeStruct(dims, dtype)


def halve(x, axis, bit):
    low = lax.axis_index(axis) & bit == 0
    keep = jnp.where(low, x[0], x[1])
    give = jnp.where(low, x[1], x[0])
    return keep, swap(give, axis, bit)


def dot(a, b, ca=1, cb=0):
    return lax.dot_general(a, b, (((ca,), (cb,)), ((), ())), preferred_element_type=F32)


STEP = 32
LANES = 128


def lanes_of(x, k):
    return x[:, k * LANES : (k + 1) * LANES]


def pack(tops, cols, out_ref, start):
    tall = len(tops) * cols
    for k in range(tops[0].shape[1] // LANES):
        rows = [lanes_of(t, k).reshape(-1, cols, LANES) for t in tops]
        rows = jnp.concatenate(rows, axis=1).astype(BF16)
        out_ref[start : start + rows.shape[0], k * tall : (k + 1) * tall] = rows


def unpack(piece, cols, blocks, b):
    tall = blocks * cols
    rows = [
        piece[:, k * tall + b * cols : k * tall + (b + 1) * cols].reshape(-1, LANES)
        for k in range(piece.shape[1] // tall)
    ]
    return jnp.concatenate(rows, axis=1)


def beside(j, part, width):
    per = width // LANES
    return pl.ds((j // per) * part, part), pl.ds((j % per) * LANES, LANES)


def weights_kernel(first_ref, second_ref, out_ref):
    blocks, part, width = first_ref.shape
    for d in range(out_ref.shape[0]):
        for b in range(blocks):
            out_ref[d, b * part : (b + 1) * part] = first_ref[b]
        for j in range(second_ref.shape[0]):
            rows, lanes = beside(j, second_ref.shape[1], width)
            out_ref[d, pl.ds(blocks * part + rows.start, rows.size), lanes] = second_ref[j]


def second_of(second_ref, j):
    nd, _, width = second_ref.shape
    rows, lanes = beside(j, LANES // nd, width)
    return second_ref[:, rows, lanes].reshape(LANES, LANES)


def rows_kernel(cols, weights_ref, x_ref, gate_ref, out_ref):
    nd, (blocks, length, width) = weights_ref.shape[0], x_ref.shape
    part = length // nd
    per = STEP * cols // part
    body = width // LANES * blocks * cols
    rider = jnp.concatenate([gate_ref[...].astype(F32)] * 2, axis=1).astype(BF16)
    for c in range(out_ref.shape[0] // STEP):
        tops = []
        for b in range(blocks):
            mine = weights_ref[c * per : (c + 1) * per, b * part : (b + 1) * part]
            tops.append(dot(mine.reshape(per * part, length), x_ref[b]))
        pack(tops, cols, out_ref, c * STEP)
        out_ref[c * STEP : (c + 1) * STEP, body:] = jnp.broadcast_to(rider[None], (STEP,) + rider.shape)


def gate_kernel(cols, x_ref, weight_ref, cot_ref, out_ref, slope_ref):
    blocks = x_ref.shape[0]
    for c in range(out_ref.shape[0] // STEP):
        rows = pl.ds(c * STEP * cols, STEP * cols)
        tops = []
        for b in range(blocks):
            gate = jax.nn.sigmoid(dot(x_ref[b, rows], weight_ref[...]))
            grad = cot_ref[b, rows].astype(F32) * gate
            slope_ref[b, rows] = grad * (1.0 - gate)
            tops.append(grad)
        pack(tops, cols, out_ref, c * STEP)


def unfold(src_ref, tmp_ref):
    tall = tmp_ref.shape[1] // src_ref.shape[0]
    for c in range(0, src_ref.shape[0], STEP):
        for k in range(tmp_ref.shape[0]):
            piece = src_ref[c : c + STEP, k * tall : (k + 1) * tall].astype(F32)
            tmp_ref[k, pl.ds(c * tall, STEP * tall)] = piece.reshape(STEP * tall, LANES)


def fold(tmp_ref, dst_ref):
    tall = tmp_ref.shape[1] // dst_ref.shape[0]
    for c in range(0, dst_ref.shape[0], STEP):
        for k in range(tmp_ref.shape[0]):
            piece = tmp_ref[k, pl.ds(c * tall, STEP * tall)].reshape(STEP, tall, LANES)
            dst_ref[c : c + STEP, k * tall : (k + 1) * tall] = piece.astype(BF16)


def column(tmp_ref, j, cols):
    rows = pl.ds(j, tmp_ref.shape[1] // cols, stride=cols)
    return jnp.concatenate([tmp_ref[k, rows] for k in range(tmp_ref.shape[0])], axis=1)


def set_column(tmp_ref, j, cols, value):
    rows = pl.ds(j, tmp_ref.shape[1] // cols, stride=cols)
    for k in range(tmp_ref.shape[0]):
        tmp_ref[k, rows] = lanes_of(value, k)


def forward_kernel(second_ref, one_ref, two_ref, by_ref, tmp_ref, res_ref):
    unfold(one_ref, tmp_ref)
    cols = by_ref.shape[0]
    for j in range(cols):
        mine = column(tmp_ref, j, cols).astype(BF16)
        by_ref[j] = mine
        set_column(res_ref, j, cols, dot(second_of(second_ref, j), mine))
    fold(res_ref, two_ref)


def backward_kernel(second_ref, grad_ref, by_ref, keep_ref, got_ref, back_ref, part_ref, tmp_ref, res_ref):
    unfold(grad_ref, tmp_ref)
    cols = by_ref.shape[0]
    nd, _, width = part_ref.shape
    for j in range(cols):
        mine = column(tmp_ref, j, cols).astype(BF16)
        set_column(res_ref, j, cols, dot(second_of(second_ref, j), mine, 0, 0))
        rows, lanes = beside(j, LANES // nd, width)
        part = dot(mine, by_ref[j], 1, 1).reshape(nd, LANES // nd, LANES)
        part_ref[:, rows, lanes] = part.astype(BF16)
    fold(res_ref, back_ref)
    body = grad_ref.shape[1]
    total = (keep_ref[...] + got_ref[...]).T
    coarse = total.astype(BF16).astype(F32)
    rider = jnp.concatenate([coarse, total - coarse], axis=1)
    rider = rider.reshape(back_ref.shape[0], back_ref.shape[1] - body, LANES)
    back_ref[:, body:] = rider.astype(BF16)


def delta_kernel(
    cols, me_ref, two_ref, slope_ref, x_ref, weight_ref, input_ref, keep_ref, give_ref, delta_ref, sum_ref
):
    blocks, length, _ = x_ref.shape
    n = STEP * cols
    for c in range(two_ref.shape[0] // STEP):
        two = two_ref[c * STEP : (c + 1) * STEP].astype(F32)
        for b in range(blocks):
            rows = pl.ds(c * n, n)
            mine = unpack(two, cols, blocks, b)
            delta_ref[b, rows] = (mine * slope_ref[b, rows]).astype(BF16)
    pairs, cpart, width = keep_ref.shape
    for b in range(blocks):
        add = dot(delta_ref[b], x_ref[b], 0, 0).reshape(pairs, 2, cpart, width)
        for k in range(2):
            sum_ref[k] = add[:, k] if b == 0 else sum_ref[k] + add[:, k]
        input_ref[b] = dot(delta_ref[b], weight_ref[...], 1, 1).astype(BF16)
    keep_ref[...] = sum_ref[me_ref[0]]
    give_ref[...] = sum_ref[1 - me_ref[0]].astype(BF16)


def outer_kernel(cols, back_ref, x_ref, second_ref, part_ref):
    blocks, length, _ = x_ref.shape
    nd, rows, width = part_ref.shape
    part = length // nd
    piece = back_ref[...].astype(F32)
    for b in range(blocks):
        mine = unpack(piece, cols, blocks, b).astype(BF16)
        add = dot(mine, x_ref[b], 1, 1).astype(BF16)
        part_ref[:, b * part : (b + 1) * part] = add.reshape(nd, part, width)
    part_ref[:, blocks * part :] = second_ref[...]


def gate_sum_kernel(riders_ref, out_ref):
    total = jnp.sum(riders_ref[...].astype(F32), axis=0)
    half = out_ref.shape[1]
    out_ref[...] = total[:, :half] + total[:, half:]


def inputs_kernel(cols, weights_ref, back_ref, input_ref, out_ref):
    nd, (blocks, length, _) = weights_ref.shape[0], out_ref.shape
    part = length // nd
    piece = back_ref[...].astype(F32)
    for b in range(blocks):
        mine = weights_ref[:, b * part : (b + 1) * part].reshape(length, length)
        through = dot(mine, unpack(piece, cols, blocks, b).astype(BF16), 0, 0)
        out_ref[b] = (through + input_ref[b].astype(F32)).astype(BF16)


def total_kernel(parts_ref, first_ref, second_ref):
    nd, _, width = parts_ref.shape
    blocks, part, _ = first_ref.shape
    for b in range(blocks):
        rows = pl.ds(b * part, part)
        first_ref[b] = sum(parts_ref[d, rows].astype(F32) for d in range(nd))
    for j in range(second_ref.shape[0]):
        rows, lanes = beside(j, second_ref.shape[1], width)
        rows = pl.ds(blocks * part + rows.start, rows.size)
        second_ref[j] = sum(parts_ref[d, rows, lanes].astype(F32) for d in range(nd))


def per_device(inputs, out_grad, first_factor, second_factor, gate_weight):
    nd = lax.axis_size(DP)
    ns = lax.axis_size(SEQ)
    ny = lax.axis_size("y")
    _, rows, width = inputs.shape
    blocks, part, length = first_factor.shape
    cols, part2, size2 = second_factor.shape
    crows, cpart = gate_weight.shape
    x = inputs.reshape(blocks, length, width)
    cot = out_grad.reshape(blocks, length, width)
    body = width // LANES * blocks * cols
    piece = shape((ns, body, LANES), BF16)
    longer = shape((ns, body + crows, LANES), BF16)
    wide = 2 * rows * width * width
    cells = pltpu.VMEM((width // LANES, rows, LANES), F32)
    tail = cols * part2 * size2 // width
    both_rows = blocks * part + tail
    by_second = pl.BlockSpec((nd, tail, width), lambda i: (0, blocks * part // tail, 0))
    by_body = pl.BlockSpec(piece.shape, lambda i: (0, 0, 0))
    by_rider = pl.BlockSpec((ns, crows, LANES), lambda i: (0, body // crows, 0))

    weights = local(
        weights_kernel, shape((nd, both_rows, width), BF16), [first_factor, second_factor]
    )
    weights = exchange(weights, DP)
    one = local(
        functools.partial(rows_kernel, cols), longer, [weights, x, gate_weight], flops=wide
    )
    col_one = exchange(one, SEQ)
    col_two, by_col = local(
        forward_kernel,
        (piece, shape((cols, size2, width), BF16)),
        [weights, col_one],
        [by_second, by_body],
        flops=wide // 4,
        scratch=[cells, cells],
    )
    col_one, col_two = lax.optimization_barrier((col_one, col_two))
    two = exchange(col_two, SEQ)

    gate_part = col_one[:, body:, :cpart].reshape(width, cpart)
    gate_full = gather(gate_part, DP).transpose(1, 0, 2).reshape(width, width)
    mixed_grad, slope = local(
        functools.partial(gate_kernel, cols),
        (piece, shape(x.shape, F32)),
        [x, gate_full, cot],
        flops=wide,
    )
    two, mixed_grad = lax.optimization_barrier((two, mixed_grad))
    col_grad = exchange(mixed_grad, SEQ)

    gate_input, keep, give = local(
        functools.partial(delta_kernel, cols),
        (
            shape(x.shape, BF16),
            shape((ny, cpart, width), F32),
            shape((ny, cpart, width), BF16),
        ),
        [lax.axis_index("xl")[None], two, slope, x, gate_full],
        [SMEM] + [VMEM] * 4,
        flops=2 * wide,
        scratch=[pltpu.VMEM(x.shape, BF16), pltpu.VMEM((2, ny, cpart, width), F32)],
    )
    gsum = keep + swap(give, "xl", 1).astype(F32)
    keep, got = halve(gsum.reshape(2, ny // 2, cpart, width), "y", 2)
    keep, got = halve(keep + got, "y", 1)
    col_grad, keep, got = lax.optimization_barrier((col_grad, keep, got))

    col_back, spart = local(
        backward_kernel,
        (longer, shape((nd, tail, width), BF16)),
        [weights, col_grad, by_col, keep, got],
        [by_second] + [VMEM] * 4,
        flops=wide // 2,
        scratch=[cells, cells],
    )
    back = exchange(col_back, SEQ)

    parts = local(
        functools.partial(outer_kernel, cols),
        shape(weights.shape, BF16),
        [back, x, spart],
        [by_body, VMEM, VMEM],
        flops=wide,
    )
    back, parts = lax.optimization_barrier((back, parts))
    parts = exchange(parts, DP)
    grad_gate = local(gate_sum_kernel, shape(gate_weight.shape, F32), [back], [by_rider])
    grad_inputs = local(
        functools.partial(inputs_kernel, cols),
        shape(x.shape, BF16),
        [weights, back, gate_input],
        [VMEM, by_body, VMEM],
        flops=wide,
    )
    grad_first, grad_second = local(
        total_kernel, (shape(first_factor.shape, F32), shape(second_factor.shape, F32)), [parts]
    )
    return (grad_inputs.reshape(inputs.shape), grad_first, grad_second, grad_gate)


def solution(mesh):
    fine = Mesh(mesh.devices.reshape(16, 2, 2, 4, 2), SEQ + DP)
    specs = (P(SEQ, DP, None), P(SEQ, DP, None), P(SEQ, DP))
    return jax.shard_map(
        per_device,
        mesh=fine,
        in_specs=(P(DP, SEQ, None), P(DP, SEQ, None)) + specs,
        out_specs=(P(DP, SEQ, None),) + specs,
        check_vma=False,
    )
```
